32 devices in a mesh: seq: 8 (over z, x), grp: 4 (over y, core).
Axes of the slice: x: 2, y: 2, z: 4, core: 2. Of those that a mesh axis runs over, the one named last changes fastest.
Arguments:
- linear_query: bfloat16 [4096, 256], P(('grp', 'seq')), parts along dimension 0, may hold values from -6 to 6
- linear_key: bfloat16 [4096, 256], P(('grp', 'seq')), parts along dimension 0, may hold values from -16 to 16
- values: bfloat16 [4096, 2048], P(('grp', 'seq')), parts along dimension 0, may hold values from -6 to 6
- window_query: bfloat16 [4096, 2048], P(('grp', 'seq')), parts along dimension 0, may hold values from -5 to 5
- window_key: bfloat16 [4096, 2048], P(('grp', 'seq')), parts along dimension 0, may hold values from -5 to 5
Outputs:
- linear_out: float32 [4096, 2048], P(('grp', 'seq')), parts along dimension 0
- window_out: bfloat16 [4096, 2048], P(('grp', 'seq')), parts along dimension 0
The draws below stay inside these ranges and needn't reach their ends.
There are 4 independent parts, one for each index of `grp`. The reference program is written for one: setup_inputs(seed, part) draws one part's arguments, and reference() takes and returns one part's arrays. A program takes and returns all parts, laid end to end along the dimension named above; each array names one. Nothing has to cross between parts.
All inputs are finite; a program needn't handle non-finite values.
Results may differ from the reference program's by a relative error of at most 0.0085.
Values may be sent and summed in bfloat16 or wider, within the bound.
A program may use at most 64 MiB of HBM per device.

```python
import math
import jax
import jax.numpy as jnp
from jax import lax

HEADS = 16
FEAT = 16
HEAD_DIM = 128
WINDOW = 256
TOKENS = 1024


def draw_linear_key(key, part):
    row_scale = jnp.exp(jax.random.uniform(jax.random.fold_in(key, 3), (TOKENS, 1), jnp.float32, math.log(0.35), math.log(3.5)))
    column_scale = jnp.exp(jax.random.uniform(jax.random.fold_in(key, 4), (1, HEADS * FEAT), jnp.float32, math.log(0.35), math.log(3.5)))
    sample = jax.random.normal(jax.random.fold_in(key, 5), (TOKENS, HEADS * FEAT), jnp.float32)
    return jnp.clip(sample * row_scale * column_scale, -16.0, 16.0).astype(jnp.bfloat16)


def draw_window_query(key, part):
    sample = jax.random.normal(jax.random.fold_in(key, 1), (TOKENS, HEADS * HEAD_DIM), jnp.float32)
    return jnp.clip(sample, -5.0, 5.0).astype(jnp.bfloat16)


def draw_window_key(key, part):
    row_scale = jnp.exp(jax.random.uniform(jax.random.fold_in(key, 6), (TOKENS, 1), jnp.float32, math.log(0.3), math.log(3.0)))
    sample = row_scale * jax.random.normal(jax.random.fold_in(key, 2), (TOKENS, HEADS * HEAD_DIM), jnp.float32)
    return jnp.clip(sample, -5.0, 5.0).astype(jnp.bfloat16)


def steps_of(key, extent, cuts, low, high):
    gain, own = 1.0, jax.random.fold_in(key, 6)
    for axis_at, parts in cuts:
        heights = jnp.exp(jax.random.uniform(jax.random.fold_in(own, axis_at), (parts,), jnp.float32, low / len(cuts), high / len(cuts)))
        gain = gain * jnp.repeat(heights, extent[axis_at] // parts).reshape([-1 if axis == axis_at else 1 for axis in range(len(extent))])
    return gain


def scatter_about(key, dims, spread, limit, pieces=(), held_as=jnp.bfloat16):
    gain = steps_of(key, dims, pieces, -0.22, 0.18) if pieces else 1.0
    values = jax.random.normal(key, dims, jnp.float32) * spread * gain
    return jnp.minimum(jnp.maximum(values, -limit), limit).astype(held_as)


def setup_inputs(seed: int = 0, part: int = 0) -> dict:
    key_list = jax.random.split(jax.random.key(seed), 6)
    part_splits = jax.random.split(jax.random.fold_in(key_list[5], part), 6)
    return {
        "linear_query": scatter_about(part_splits[0], (TOKENS, HEADS * FEAT), 1.0, 6.0, ((0, 8),)),
        "linear_key": draw_linear_key(jax.random.fold_in(jax.random.fold_in(key_list[5], part), 71), part),
        "values": scatter_about(part_splits[2], (TOKENS, HEADS * HEAD_DIM), 1.0, 6.0, ((0, 8),)),
        "window_query": draw_window_query(jax.random.fold_in(jax.random.fold_in(key_list[5], part), 71), part),
        "window_key": draw_window_key(jax.random.fold_in(jax.random.fold_in(key_list[5], part), 71), part),
    }


PRECISE = lax.Precision.HIGHEST
HALF_ROOT = 0.7071067811865476


def full_features(scaled):
    row_count, head_count, feat_count = scaled.shape
    columns = jnp.transpose(scaled, (1, 2, 0))
    outer_prod = (columns[:, :, None, :] * columns[:, None, :, :] * HALF_ROOT).reshape(head_count, feat_count * feat_count, row_count)
    return jnp.concatenate([jnp.ones((head_count, 1, row_count), jnp.float32), columns, outer_prod], axis=1)


def reference(linear_query, linear_key, values, window_query, window_key):
    token_count = values.shape[0]
    head_count = linear_query.shape[1] // FEAT
    value_width = values.shape[1] // head_count
    block_size = math.gcd(token_count, 512)
    block_count = token_count // block_size
    feat_total = 1 + FEAT + FEAT * FEAT
    query_scaled = (linear_query.astype(jnp.float32) * FEAT ** -0.25).reshape(block_count, block_size, head_count, FEAT)
    key_scaled = (linear_key.astype(jnp.float32) * FEAT ** -0.25).reshape(block_count, block_size, head_count, FEAT)
    value_heads = values.astype(jnp.float32).reshape(block_count, block_size, head_count, value_width)
    causal = jnp.arange(block_size)[:, None] >= jnp.arange(block_size)[None, :]

    def advance(running, block_data):
        state, normer = running
        query_block, key_block, value_block = block_data
        query_feats = full_features(query_block)
        key_feats = full_features(key_block)
        inner_prod = jnp.einsum("thf,jhf->htj", query_block, key_block, precision=PRECISE)
        kernel = jnp.where(causal[None], 1.0 + inner_prod + 0.5 * inner_prod * inner_prod, 0.0)
        numerator = jnp.einsum("htj,jhv->thv", kernel, value_block, precision=PRECISE) + jnp.einsum("hpt,hpv->thv", query_feats, state, precision=PRECISE)
        denominator = jnp.sum(kernel, axis=2).T + jnp.einsum("hpt,hp->th", query_feats, normer, precision=PRECISE)
        state = state + jnp.einsum("hpr,rhv->hpv", key_feats, value_block, precision=PRECISE)
        normer = normer + jnp.sum(key_feats, axis=2)
        return (state, normer), numerator / denominator[:, :, None]

    initial = (jnp.zeros((head_count, feat_total, value_width), jnp.float32), jnp.zeros((head_count, feat_total), jnp.float32))
    unused, blocks = lax.scan(advance, initial, (query_scaled, key_scaled, value_heads))
    linear_out = blocks.reshape(token_count, head_count * value_width)

    width = values.shape[1]
    pad_keys = jnp.concatenate([jnp.zeros((WINDOW, width), window_key.dtype), window_key], axis=0)
    pad_values = jnp.concatenate([jnp.zeros((WINDOW, width), values.dtype), values], axis=0)

    def attend(block_index):
        begin = (block_index * block_size).astype(jnp.int32)
        query_block = lax.dynamic_slice_in_dim(window_query, begin, block_size, 0).astype(jnp.float32)
        key_block = lax.dynamic_slice_in_dim(pad_keys, begin, block_size + WINDOW, 0).astype(jnp.float32)
        value_block = lax.dynamic_slice_in_dim(pad_values, begin, block_size + WINDOW, 0).astype(jnp.float32)
        query_pos = begin + jnp.arange(block_size, dtype=jnp.int32)
        key_pos = begin - WINDOW + jnp.arange(block_size + WINDOW, dtype=jnp.int32)
        allowed = (key_pos[None, :] <= query_pos[:, None]) & (key_pos[None, :] > query_pos[:, None] - WINDOW) & (key_pos[None, :] >= 0)
        scores = jnp.einsum("thd,jhd->htj", query_block.reshape(block_size, head_count, value_width), key_block.reshape(block_size + WINDOW, head_count, value_width)) * HEAD_DIM ** -0.5
        masked = jnp.where(allowed[None], scores, -jnp.inf)
        largest = jnp.max(masked, axis=2, keepdims=True)
        exponent = jnp.exp(masked - largest)
        weights = (exponent / jnp.sum(exponent, axis=2, keepdims=True)).astype(jnp.bfloat16)
        mixed = jnp.einsum("htj,jhv->thv", weights.astype(jnp.float32), value_block.reshape(block_size + WINDOW, head_count, value_width))
        return mixed.astype(jnp.bfloat16).reshape(block_size, width)

    window_blocks = lax.map(attend, jnp.arange(block_count, dtype=jnp.int32))
    window_out = window_blocks.reshape(token_count, width)
    return (linear_out, window_out)
```

```python
import functools
import jax
import jax.numpy as jnp
import numpy as np
from jax import lax
from jax.experimental import pallas as pl
from jax.experimental.pallas import tpu as pltpu
from jax.sharding import PartitionSpec as P

FEAT = 16
WINDOW = 256
PAIRS = FEAT * (FEAT + 1) // 2
FEATS = 160
ONE_ROW = PAIRS + FEAT
CHUNKS = 4
MESH = pl.DeviceIdType.MESH
F32 = jnp.float32
BF16 = jnp.bfloat16


def selections(lanes):
    lower, upper = np.triu_indices(FEAT)
    left = np.zeros((FEATS, FEAT), np.float32)
    right = np.zeros((FEATS, FEAT), np.float32)
    right_query = np.zeros((FEATS, FEAT), np.float32)
    rows = np.arange(PAIRS)
    left[rows, lower] = 1.0
    right[rows, upper] = 1.0
    right_query[rows, upper] = np.where(lower == upper, 1.0, 2.0)
    left[PAIRS + np.arange(FEAT), np.arange(FEAT)] = 1.0
    stacked = np.stack([left, right, right_query])
    return jnp.asarray(np.tile(stacked, (1, 1, lanes // FEAT)), BF16)


def dot_t(a, b):
    return lax.dot_general(a, b, (((1,), (1,)), ((), ())), preferred_element_type=F32)


def dot(a, b):
    return jnp.dot(a, b, preferred_element_type=F32)


def kernel(
    pairs, rows, dim, heads,
    lq_ref, lk_ref, v_ref, wq_ref, wk_ref, sel_ref,
    lin_ref, win_ref,
    lq2, lk2, v2, q2, k2, pv, pk, num, den, state, norm, state_in, norm_in, state_out, norm_out,
    lin_f, lin_b, win_b, lin_in, win_in,
    xs, xr, zs, zr, ys, yr, cs, cr, rs, rr,
):
    me = lax.axis_index("seq")
    pair = me // 2
    par = me % 2
    other = 1 - par
    partner = {"seq": pair * 2 + other}
    ahead = {"seq": jnp.minimum(me + 2, 2 * pairs - 1)}
    behind = {"seq": jnp.maximum(me - 2, 0)}
    has_next = pair < pairs - 1
    has_prev = pair > 0
    half_heads = heads // 2
    half = half_heads * dim
    width = half // CHUNKS
    per = width // dim
    lanes = half_heads * FEAT
    mine = pl.ds(pl.multiple_of(par * rows, rows), rows)
    theirs = pl.ds(pl.multiple_of(other * rows, rows), rows)

    def own_cols(c):
        return pl.ds(pl.multiple_of(par * half + c * width, width), width)

    def other_cols(c):
        return pl.ds(pl.multiple_of(other * half + c * width, width), width)

    def cols(c):
        return pl.ds(c * width if isinstance(c, int) else pl.multiple_of(c * width, width), width)

    barrier = pltpu.get_barrier_semaphore()
    pl.semaphore_signal(barrier, inc=1, device_id=partner, device_id_type=MESH)

    @pl.when(has_next)
    def _():
        pl.semaphore_signal(barrier, inc=1, device_id=ahead, device_id_type=MESH)

    @pl.when(has_prev)
    def _():
        pl.semaphore_signal(barrier, inc=1, device_id=behind, device_id_type=MESH)

    pl.semaphore_wait(barrier, 1 + jnp.minimum(pair, 1) + jnp.minimum(pairs - 1 - pair, 1))

    def remote(src, dst, send, recv, where):
        return pltpu.make_async_remote_copy(
            src_ref=src, dst_ref=dst, send_sem=send, recv_sem=recv,
            device_id=where, device_id_type=MESH,
        )

    small_other = pl.ds(pl.multiple_of(other * lanes, lanes), lanes)
    small_own = pl.ds(pl.multiple_of(par * lanes, lanes), lanes)

    def x_lk():
        return remote(lk_ref.at[:, small_other], lk2.at[mine, :], xs.at[0], xr.at[0], partner)

    def x_lq():
        return remote(lq_ref.at[:, small_other], lq2.at[mine, :], xs.at[1], xr.at[1], partner)

    def x_copy(src, dst, slot, c):
        at = 2 + slot * CHUNKS + c
        return remote(src.at[:, other_cols(c)], dst.at[mine, cols(c)], xs.at[at], xr.at[at], partner)

    def x_v(c):
        return x_copy(v_ref, v2, 0, c)

    def x_k(c):
        return x_copy(wk_ref, k2, 1, c)

    def x_q(c):
        return x_copy(wq_ref, q2, 2, c)

    def z_v(c):
        return remote(v_ref.at[:, own_cols(c)], pv.at[mine, cols(c)], zs.at[c], zr.at[c], ahead)

    def z_k(c):
        at = CHUNKS + c
        return remote(wk_ref.at[:, own_cols(c)], pk.at[mine, cols(c)], zs.at[at], zr.at[at], ahead)

    def y_v(c):
        return remote(v2.at[theirs, cols(c)], pv.at[theirs, cols(c)], ys.at[c], yr.at[c], ahead)

    def y_k(c):
        at = CHUNKS + c
        return remote(k2.at[theirs, cols(c)], pk.at[theirs, cols(c)], ys.at[at], yr.at[at], ahead)

    def c_state(c):
        return remote(state_out.at[c], state_in.at[c], cs.at[c], cr.at[c], ahead)

    def c_norm():
        return remote(norm_out, norm_in, cs.at[CHUNKS], cr.at[CHUNKS], ahead)

    def r_lin(c):
        return remote(lin_b.at[theirs, cols(c)], lin_in.at[:, cols(c)], rs.at[c], rr.at[c], partner)

    def r_win(c):
        at = CHUNKS + c
        return remote(win_b.at[theirs, cols(c)], win_in.at[:, cols(c)], rs.at[at], rr.at[at], partner)

    x_lk().start()
    x_lq().start()
    for c in range(CHUNKS):
        x_v(c).start()
        x_k(c).start()

        @pl.when(has_next)
        def _():
            z_v(c).start()
            z_k(c).start()

    for c in range(CHUNKS):
        x_q(c).start()

    lq2[mine, :] = lq_ref[:, small_own]
    lk2[mine, :] = lk_ref[:, small_own]
    for c in range(CHUNKS):
        v2[mine, cols(c)] = v_ref[:, own_cols(c)]
        k2[mine, cols(c)] = wk_ref[:, own_cols(c)]
        q2[mine, cols(c)] = wq_ref[:, own_cols(c)]

    @pl.when(pair == 0)
    def _():
        pv[...] = jnp.zeros_like(pv)
        pk[...] = jnp.zeros_like(pk)
        state_in[...] = jnp.zeros_like(state_in)
        norm_in[...] = jnp.zeros_like(norm_in)

    norm[...] = jnp.zeros_like(norm)
    x_lk().wait_recv()
    x_lq().wait_recv()

    both = 2 * rows
    ones = jnp.ones((both, dim), BF16)
    lane = lax.broadcasted_iota(jnp.int32, (both, lanes), 1) // FEAT
    row_at = lax.broadcasted_iota(jnp.int32, (both, both), 0)
    col_at = lax.broadcasted_iota(jnp.int32, (both, both), 1)
    causal = col_at <= row_at
    feat_row = lax.broadcasted_iota(jnp.int32, (FEATS, both), 0)
    row_left = jnp.where(feat_row == ONE_ROW, 1.0, 0.0)
    row_right = jnp.where((feat_row >= PAIRS) & (feat_row <= ONE_ROW), 1.0, 0.0)
    norm_lane = lax.broadcasted_iota(jnp.int32, (FEATS, 128), 1)

    def first(c, carry):
        x_v(c).wait_recv()
        x_k(c).wait_recv()

        @pl.when(has_next)
        def _():
            y_v(c).start()
            y_k(c).start()

        for u in range(per):
            head = c * per + u
            at = pl.ds(pl.multiple_of(head * dim, dim), dim)
            chosen = lane == head
            keys = lk2[...]
            key_m = jnp.where(chosen, keys.astype(F32), 0.0).astype(BF16)
            query_m = jnp.where(chosen, lq2[...].astype(F32) * 0.25, 0.0).astype(BF16)
            values = jnp.concatenate([v2[:, at], ones], axis=1)
            feats = (dot_t(sel_ref[0], key_m) + row_left) * (dot_t(sel_ref[1], key_m) + row_right)
            summed = dot(feats.astype(BF16), values)
            state[head] = summed[:, :dim]
            norm[...] += jnp.where(norm_lane == head, summed[:, dim:], 0.0)
            a = dot_t(query_m, keys) + 1.0
            weight = jnp.where(causal, a * a + 1.0, 0.0).astype(BF16)
            mixed = dot(weight, values)
            num[:, at] = mixed[:, :dim]
            den[:, at] = mixed[:, dim:]
        return carry

    lax.fori_loop(0, CHUNKS, first, 0)

    @pl.when(has_prev)
    def _():
        c_norm().wait_recv()

    @pl.when(has_next)
    def _():
        norm_out[...] = norm_in[...] + norm[...]
        c_norm().start()

    def chain(c, carry):
        @pl.when(has_prev)
        def _():
            c_state(c).wait_recv()

        @pl.when(has_next)
        def _():
            total = state_in[c].astype(F32) + state[pl.ds(c * per, per)]
            state_out[c] = total.astype(state_out.dtype)
            c_state(c).start()

        return carry

    lax.fori_loop(0, CHUNKS, chain, 0)

    span = 3 * rows
    q_at = lax.broadcasted_iota(jnp.int32, (rows, span), 0)
    k_at = lax.broadcasted_iota(jnp.int32, (rows, span), 1)
    band = (k_at > q_at) & (k_at <= q_at + both)
    empty = jnp.where(pair == 0, 1, 0)
    factor = dim ** -0.5 * 1.4426950408889634
    feat_lane = lax.broadcasted_iota(jnp.int32, (both, FEATS), 1)
    lane_left = jnp.where(feat_lane == ONE_ROW, 1.0, 0.0)
    lane_right = jnp.where((feat_lane >= PAIRS) & (feat_lane <= ONE_ROW), 2.0, 0.0)
    wide_ones = jnp.ones((span, dim), BF16)

    def second(c, carry):
        x_q(c).wait_recv()

        @pl.when(has_prev)
        def _():
            z_v(c).wait_recv()
            z_k(c).wait_recv()
            y_v(c).wait_recv()
            y_k(c).wait_recv()

        for u in range(per):
            head = c * per + u
            at = pl.ds(pl.multiple_of(head * dim, dim), dim)
            for part in range(2):
                begin = part * rows
                keys = jnp.concatenate([pk[begin:, at], k2[: begin + rows, at]], axis=0)
                values = jnp.concatenate([pv[begin:, at], v2[: begin + rows, at]], axis=0)
                scores = dot_t(q2[begin : begin + rows, at], keys) * factor
                allowed = band & (k_at >= empty * (both - begin))
                scores = jnp.where(allowed, scores, -1e30)
                largest = jnp.max(scores, axis=1, keepdims=True)
                weight = jnp.exp2(scores - largest).astype(BF16)
                mixed = dot(weight, jnp.concatenate([values, wide_ones], axis=1))
                win_b[begin : begin + rows, at] = (mixed[:, :dim] / mixed[:, dim:]).astype(BF16)

            query_m = jnp.where(lane == head, lq2[...].astype(F32) * 0.25, 0.0).astype(BF16)
            feats = (dot_t(query_m, sel_ref[0]) + lane_left) * (dot_t(query_m, sel_ref[2]) + lane_right)
            norm_col = jnp.sum(jnp.where(norm_lane == head, norm_in[...], 0.0), axis=1, keepdims=True)
            prior = jnp.concatenate(
                [state_in[c, u].astype(BF16), jnp.broadcast_to(norm_col, (FEATS, dim)).astype(BF16)], axis=1
            )
            added = dot(feats.astype(BF16), prior)
            linear = (num[:, at] + added[:, :dim]) / (den[:, at] + added[:, dim:])
            lin_f[:, at] = linear
            lin_b[:, at] = linear.astype(BF16)
        r_lin(c).start()
        r_win(c).start()
        win_ref[:, own_cols(c)] = win_b[mine, cols(c)]
        lin_ref[:, own_cols(c)] = lin_f[mine, cols(c)]
        return carry

    lax.fori_loop(0, CHUNKS, second, 0)

    def last(c, carry):
        r_lin(c).wait_recv()
        r_win(c).wait_recv()
        win_ref[:, other_cols(c)] = win_in[:, cols(c)]
        lin_ref[:, other_cols(c)] = lin_in[:, cols(c)].astype(F32)
        return carry

    lax.fori_loop(0, CHUNKS, last, 0)

    x_lk().wait_send()
    x_lq().wait_send()
    for c in range(CHUNKS):
        x_v(c).wait_send()
        x_k(c).wait_send()
        x_q(c).wait_send()
        r_lin(c).wait_send()
        r_win(c).wait_send()

    @pl.when(has_next)
    def _():
        c_norm().wait_send()
        for c in range(CHUNKS):
            z_v(c).wait_send()
            z_k(c).wait_send()
            y_v(c).wait_send()
            y_k(c).wait_send()
            c_state(c).wait_send()


def on_device(linear_query, linear_key, values, window_query, window_key):
    rows, width = values.shape
    heads = linear_query.shape[1] // FEAT
    dim = width // heads
    pairs = lax.axis_size("seq") // 2
    half_heads = heads // 2
    half = width // 2
    lanes = half_heads * FEAT
    both = 2 * rows
    per = half_heads // CHUNKS
    state_type = BF16 if pairs <= 8 else F32
    vmem = pl.BlockSpec(memory_space=pltpu.VMEM)
    dma = pltpu.SemaphoreType.DMA
    return pl.pallas_call(
        functools.partial(kernel, pairs, rows, dim, heads),
        out_shape=(
            jax.ShapeDtypeStruct((rows, width), F32),
            jax.ShapeDtypeStruct((rows, width), BF16),
        ),
        in_specs=[vmem] * 6,
        out_specs=(vmem, vmem),
        scratch_shapes=[
            pltpu.VMEM((both, lanes), BF16),
            pltpu.VMEM((both, lanes), BF16),
            pltpu.VMEM((both, half), BF16),
            pltpu.VMEM((both, half), BF16),
            pltpu.VMEM((both, half), BF16),
            pltpu.VMEM((both, half), BF16),
            pltpu.VMEM((both, half), BF16),
            pltpu.VMEM((both, half), F32),
            pltpu.VMEM((both, half), F32),
            pltpu.VMEM((half_heads, FEATS, dim), F32),
            pltpu.VMEM((FEATS, 128), F32),
            pltpu.VMEM((CHUNKS, per, FEATS, dim), state_type),
            pltpu.VMEM((FEATS, 128), F32),
            pltpu.VMEM((CHUNKS, per, FEATS, dim), state_type),
            pltpu.VMEM((FEATS, 128), F32),
            pltpu.VMEM((both, half), F32),
            pltpu.VMEM((both, half), BF16),
            pltpu.VMEM((both, half), BF16),
            pltpu.VMEM((rows, half), BF16),
            pltpu.VMEM((rows, half), BF16),
            dma((2 + 3 * CHUNKS,)),
            dma((2 + 3 * CHUNKS,)),
            dma((2 * CHUNKS,)),
            dma((2 * CHUNKS,)),
            dma((2 * CHUNKS,)),
            dma((2 * CHUNKS,)),
            dma((CHUNKS + 1,)),
            dma((CHUNKS + 1,)),
            dma((2 * CHUNKS,)),
            dma((2 * CHUNKS,)),
        ],
        compiler_params=pltpu.CompilerParams(
            collective_id=0, has_side_effects=True, vmem_limit_bytes=48 * 1024 * 1024
        ),
        cost_estimate=pl.CostEstimate(
            flops=4_000_000_000, bytes_accessed=4_000_000, transcendentals=1_600_000
        ),
    )(linear_query, linear_key, values, window_query, window_key, selections(lanes))


def solution(mesh):
    spec = P(("grp", "seq"), None)
    return jax.shard_map(
        on_device,
        mesh=mesh,
        in_specs=(spec,) * 5,
        out_specs=(spec, spec),
        check_vma=False,
    )
```

```python
import functools
import jax
import jax.numpy as jnp
import numpy as np
from jax import lax
from jax.experimental import pallas as pl
from jax.experimental.pallas import tpu as pltpu
from jax.sharding import PartitionSpec as P

FEAT = 16
WINDOW = 256
PAIRS = FEAT * (FEAT + 1) // 2
FEATS = 160
ONE_ROW = PAIRS + FEAT
CHUNKS = 4
MESH = pl.DeviceIdType.MESH
F32 = jnp.float32
BF16 = jnp.bfloat16


def selections(lanes):
    lower, upper = np.triu_indices(FEAT)
    left = np.zeros((FEATS, FEAT), np.float32)
    right = np.zeros((FEATS, FEAT), np.float32)
    right_query = np.zeros((FEATS, FEAT), np.float32)
    rows = np.arange(PAIRS)
    left[rows, lower] = 1.0
    right[rows, upper] = 1.0
    right_query[rows, upper] = np.where(lower == upper, 1.0, 2.0)
    left[PAIRS + np.arange(FEAT), np.arange(FEAT)] = 1.0
    stacked = np.stack([left, right, right_query])
    return jnp.asarray(np.tile(stacked, (1, 1, lanes // FEAT)), BF16)


def dot_t(a, b):
    return lax.dot_general(a, b, (((1,), (1,)), ((), ())), preferred_element_type=F32)


def dot(a, b):
    return jnp.dot(a, b, preferred_element_type=F32)


def kernel(
    pairs, rows, dim, heads,
    lq_ref, lk_ref, v_ref, wq_ref, wk_ref, sel_in,
    lin_ref, win_ref,
    sel_ref, lq2, lk2, v2, q2, k2, pv, pk, num, den, state, norm, state_in, norm_in, state_out, norm_out,
    lin_f, lin_b, win_b, lin_in, win_in,
    xs, xr, zs, zr, ys, yr, cs, cr, rs, rr, ls,
):
    me = lax.axis_index("seq")
    pair = me // 2
    par = me % 2
    other = 1 - par
    partner = {"seq": pair * 2 + other}
    ahead = {"seq": jnp.minimum(me + 2, 2 * pairs - 1)}
    behind = {"seq": jnp.maximum(me - 2, 0)}
    has_next = pair < pairs - 1
    has_prev = pair > 0
    half_heads = heads // 2
    half = half_heads * dim
    width = half // CHUNKS
    per = width // dim
    lanes = half_heads * FEAT
    mine = pl.ds(pl.multiple_of(par * rows, rows), rows)
    theirs = pl.ds(pl.multiple_of(other * rows, rows), rows)

    def own_cols(c):
        return pl.ds(pl.multiple_of(par * half + c * width, width), width)

    def other_cols(c):
        return pl.ds(pl.multiple_of(other * half + c * width, width), width)

    def cols(c):
        return pl.ds(c * width if isinstance(c, int) else pl.multiple_of(c * width, width), width)

    barrier = pltpu.get_barrier_semaphore()
    pl.semaphore_signal(barrier, inc=1, device_id=partner, device_id_type=MESH)

    @pl.when(has_next)
    def _():
        pl.semaphore_signal(barrier, inc=1, device_id=ahead, device_id_type=MESH)

    @pl.when(has_prev)
    def _():
        pl.semaphore_signal(barrier, inc=1, device_id=behind, device_id_type=MESH)

    pl.semaphore_wait(barrier, 1 + jnp.minimum(pair, 1) + jnp.minimum(pairs - 1 - pair, 1))

    def remote(src, dst, send, recv, where):
        return pltpu.make_async_remote_copy(
            src_ref=src, dst_ref=dst, send_sem=send, recv_sem=recv,
            device_id=where, device_id_type=MESH,
        )

    small_other = pl.ds(pl.multiple_of(other * lanes, lanes), lanes)
    small_own = pl.ds(pl.multiple_of(par * lanes, lanes), lanes)

    def x_lk():
        return remote(lk_ref.at[:, small_other], lk2.at[mine, :], xs.at[0], xr.at[0], partner)

    def x_lq():
        return remote(lq_ref.at[:, small_other], lq2.at[mine, :], xs.at[1], xr.at[1], partner)

    def x_copy(src, dst, slot, c):
        at = 2 + slot * CHUNKS + c
        return remote(src.at[:, other_cols(c)], dst.at[mine, cols(c)], xs.at[at], xr.at[at], partner)

    def x_v(c):
        return x_copy(v_ref, v2, 0, c)

    def x_k(c):
        return x_copy(wk_ref, k2, 1, c)

    def x_q(c):
        return x_copy(wq_ref, q2, 2, c)

    def z_v(c):
        return remote(v_ref.at[:, own_cols(c)], pv.at[mine, cols(c)], zs.at[c], zr.at[c], ahead)

    def z_k(c):
        at = CHUNKS + c
        return remote(wk_ref.at[:, own_cols(c)], pk.at[mine, cols(c)], zs.at[at], zr.at[at], ahead)

    def y_v(c):
        return remote(v2.at[theirs, cols(c)], pv.at[theirs, cols(c)], ys.at[c], yr.at[c], ahead)

    def y_k(c):
        at = CHUNKS + c
        return remote(k2.at[theirs, cols(c)], pk.at[theirs, cols(c)], ys.at[at], yr.at[at], ahead)

    def c_state(c):
        return remote(state_out.at[c], state_in.at[c], cs.at[c], cr.at[c], ahead)

    def c_norm():
        return remote(norm_out, norm_in, cs.at[CHUNKS], cr.at[CHUNKS], ahead)

    def r_lin(c):
        return remote(lin_b.at[theirs, cols(c)], lin_in.at[:, cols(c)], rs.at[c], rr.at[c], partner)

    def r_win(c):
        at = CHUNKS + c
        return remote(win_b.at[theirs, cols(c)], win_in.at[:, cols(c)], rs.at[at], rr.at[at], partner)

    def local(src, dst, at):
        return pltpu.make_async_copy(src, dst, ls.at[at])

    def z_own(c):
        z_v(c).start()
        z_k(c).start()

    x_lk().start()
    x_lq().start()
    for c in range(CHUNKS):
        x_v(c).start()

    @pl.when(has_next)
    def _():
        z_own(0)

        @pl.when(has_prev)
        def _():
            z_own(1)

    small = [
        local(sel_in, sel_ref, 0),
        local(lk_ref.at[:, small_own], lk2.at[mine, :], 1),
        local(lq_ref.at[:, small_own], lq2.at[mine, :], 2),
    ]
    all_own = pl.ds(pl.multiple_of(par * half, half), half)
    large = [
        local(v_ref.at[:, all_own], v2.at[mine, :], 3),
        local(wk_ref.at[:, all_own], k2.at[mine, :], 4),
        local(wq_ref.at[:, all_own], q2.at[mine, :], 5),
    ]
    for copy in small + large:
        copy.start()
    for c in range(CHUNKS):
        x_k(c).start()
    for c in range(CHUNKS):
        x_q(c).start()

    @pl.when(pair == 0)
    def _():
        pv[...] = jnp.zeros_like(pv)
        pk[...] = jnp.zeros_like(pk)
        state_in[...] = jnp.zeros_like(state_in)
        norm_in[...] = jnp.zeros_like(norm_in)

    norm[...] = jnp.zeros_like(norm)
    for copy in small + large:
        copy.wait()
    x_lk().wait_recv()
    x_lq().wait_recv()

    both = 2 * rows
    ones = jnp.ones((both, dim), BF16)
    lane = lax.broadcasted_iota(jnp.int32, (both, lanes), 1) // FEAT
    row_at = lax.broadcasted_iota(jnp.int32, (both, both), 0)
    col_at = lax.broadcasted_iota(jnp.int32, (both, both), 1)
    causal = col_at <= row_at
    feat_row = lax.broadcasted_iota(jnp.int32, (FEATS, both), 0)
    row_left = jnp.where(feat_row == ONE_ROW, 1.0, 0.0)
    row_right = jnp.where((feat_row >= PAIRS) & (feat_row <= ONE_ROW), 1.0, 0.0)
    norm_lane = lax.broadcasted_iota(jnp.int32, (FEATS, 128), 1)

    def first(c, carry):
        x_v(c).wait_recv()
        for u in range(per):
            head = c * per + u
            at = pl.ds(pl.multiple_of(head * dim, dim), dim)
            chosen = lane == head
            keys = lk2[...]
            key_m = jnp.where(chosen, keys.astype(F32), 0.0).astype(BF16)
            query_m = jnp.where(chosen, lq2[...].astype(F32) * 0.25, 0.0).astype(BF16)
            values = jnp.concatenate([v2[:, at], ones], axis=1)
            feats = (dot_t(sel_ref[0], key_m) + row_left) * (dot_t(sel_ref[1], key_m) + row_right)
            summed = dot(feats.astype(BF16), values)
            state[head] = summed[:, :dim]
            norm[...] += jnp.where(norm_lane == head, summed[:, dim:], 0.0)
            a = dot_t(query_m, keys) + 1.0
            weight = jnp.where(causal, a * a + 1.0, 0.0).astype(BF16)
            mixed = dot(weight, values)
            num[:, at] = mixed[:, :dim]
            den[:, at] = mixed[:, dim:]

        @pl.when(has_prev)
        def _():
            c_state(c).wait_recv()

        @pl.when(has_next)
        def _():
            total = state_in[c].astype(F32) + state[pl.ds(c * per, per)]
            state_out[c] = total.astype(state_out.dtype)
            c_state(c).start()

        return carry

    lax.fori_loop(0, CHUNKS, first, 0)

    @pl.when(has_prev)
    def _():
        c_norm().wait_recv()

    @pl.when(has_next)
    def _():
        norm_out[...] = norm_in[...] + norm[...]
        c_norm().start()

    def relay(c):
        x_k(c).wait_recv()

        @pl.when(has_next)
        def _():
            y_v(c).start()
            y_k(c).start()

    relay(0)

    @pl.when(has_next & (pair == 0))
    def _():
        z_own(1)

    relay(1)
    for c in range(2, CHUNKS):

        @pl.when(has_next)
        def _():
            z_own(c)

        relay(c)

    span = 3 * rows
    q_at = lax.broadcasted_iota(jnp.int32, (rows, span), 0)
    k_at = lax.broadcasted_iota(jnp.int32, (rows, span), 1)
    band = (k_at > q_at) & (k_at <= q_at + both)
    empty = jnp.where(pair == 0, 1, 0)
    factor = dim ** -0.5 * 1.4426950408889634
    feat_lane = lax.broadcasted_iota(jnp.int32, (both, FEATS), 1)
    lane_left = jnp.where(feat_lane == ONE_ROW, 1.0, 0.0)
    lane_right = jnp.where((feat_lane >= PAIRS) & (feat_lane <= ONE_ROW), 2.0, 0.0)
    wide_ones = jnp.ones((span, dim), BF16)

    def second(c, carry):
        x_q(c).wait_recv()

        @pl.when(has_prev)
        def _():
            z_v(c).wait_recv()
            z_k(c).wait_recv()
            y_v(c).wait_recv()
            y_k(c).wait_recv()

        for u in range(per):
            head = c * per + u
            at = pl.ds(pl.multiple_of(head * dim, dim), dim)
            for part in range(2):
                begin = part * rows
                keys = jnp.concatenate([pk[begin:, at], k2[: begin + rows, at]], axis=0)
                values = jnp.concatenate([pv[begin:, at], v2[: begin + rows, at]], axis=0)
                scores = dot_t(q2[begin : begin + rows, at], keys) * factor
                allowed = band & (k_at >= empty * (both - begin))
                scores = jnp.where(allowed, scores, -1e30)
                largest = jnp.max(scores, axis=1, keepdims=True)
                weight = jnp.exp2(scores - largest).astype(BF16)
                mixed = dot(weight, jnp.concatenate([values, wide_ones], axis=1))
                win_b[begin : begin + rows, at] = (mixed[:, :dim] / mixed[:, dim:]).astype(BF16)

            query_m = jnp.where(lane == head, lq2[...].astype(F32) * 0.25, 0.0).astype(BF16)
            feats = (dot_t(query_m, sel_ref[0]) + lane_left) * (dot_t(query_m, sel_ref[2]) + lane_right)
            norm_col = jnp.sum(jnp.where(norm_lane == head, norm_in[...], 0.0), axis=1, keepdims=True)
            prior = jnp.concatenate(
                [state_in[c, u].astype(BF16), jnp.broadcast_to(norm_col, (FEATS, dim)).astype(BF16)], axis=1
            )
            added = dot(feats.astype(BF16), prior)
            linear = (num[:, at] + added[:, :dim]) / (den[:, at] + added[:, dim:])
            lin_f[:, at] = linear
            lin_b[:, at] = linear.astype(BF16)
        r_lin(c).start()
        r_win(c).start()
        win_ref[:, own_cols(c)] = win_b[mine, cols(c)]
        lin_ref[:, own_cols(c)] = lin_f[mine, cols(c)]
        return carry

    lax.fori_loop(0, CHUNKS, second, 0)

    def last(c, carry):
        r_lin(c).wait_recv()
        r_win(c).wait_recv()
        win_ref[:, other_cols(c)] = win_in[:, cols(c)]
        lin_ref[:, other_cols(c)] = lin_in[:, cols(c)].astype(F32)
        return carry

    lax.fori_loop(0, CHUNKS, last, 0)

    x_lk().wait_send()
    x_lq().wait_send()
    for c in range(CHUNKS):
        x_v(c).wait_send()
        x_k(c).wait_send()
        x_q(c).wait_send()
        r_lin(c).wait_send()
        r_win(c).wait_send()

    @pl.when(has_next)
    def _():
        c_norm().wait_send()
        for c in range(CHUNKS):
            z_v(c).wait_send()
            z_k(c).wait_send()
            y_v(c).wait_send()
            y_k(c).wait_send()
            c_state(c).wait_send()


def on_device(linear_query, linear_key, values, window_query, window_key):
    rows, width = values.shape
    heads = linear_query.shape[1] // FEAT
    dim = width // heads
    pairs = lax.axis_size("seq") // 2
    half_heads = heads // 2
    half = width // 2
    lanes = half_heads * FEAT
    both = 2 * rows
    per = half_heads // CHUNKS
    state_type = BF16 if pairs <= 8 else F32
    vmem = pl.BlockSpec(memory_space=pltpu.VMEM)
    dma = pltpu.SemaphoreType.DMA
    return pl.pallas_call(
        functools.partial(kernel, pairs, rows, dim, heads),
        out_shape=(
            jax.ShapeDtypeStruct((rows, width), F32),
            jax.ShapeDtypeStruct((rows, width), BF16),
        ),
        in_specs=[pl.BlockSpec(memory_space=pl.ANY)] * 6,
        out_specs=(vmem, vmem),
        scratch_shapes=[
            pltpu.VMEM((3, FEATS, lanes), BF16),
            pltpu.VMEM((both, lanes), BF16),
            pltpu.VMEM((both, lanes), BF16),
            pltpu.VMEM((both, half), BF16),
            pltpu.VMEM((both, half), BF16),
            pltpu.VMEM((both, half), BF16),
            pltpu.VMEM((both, half), BF16),
            pltpu.VMEM((both, half), BF16),
            pltpu.VMEM((both, half), F32),
            pltpu.VMEM((both, half), F32),
            pltpu.VMEM((half_heads, FEATS, dim), F32),
            pltpu.VMEM((FEATS, 128), F32),
            pltpu.VMEM((CHUNKS, per, FEATS, dim), state_type),
            pltpu.VMEM((FEATS, 128), F32),
            pltpu.VMEM((CHUNKS, per, FEATS, dim), state_type),
            pltpu.VMEM((FEATS, 128), F32),
            pltpu.VMEM((both, half), F32),
            pltpu.VMEM((both, half), BF16),
            pltpu.VMEM((both, half), BF16),
            pltpu.VMEM((rows, half), BF16),
            pltpu.VMEM((rows, half), BF16),
            dma((2 + 3 * CHUNKS,)),
            dma((2 + 3 * CHUNKS,)),
            dma((2 * CHUNKS,)),
            dma((2 * CHUNKS,)),
            dma((2 * CHUNKS,)),
            dma((2 * CHUNKS,)),
            dma((CHUNKS + 1,)),
            dma((CHUNKS + 1,)),
            dma((2 * CHUNKS,)),
            dma((2 * CHUNKS,)),
            dma((6,)),
        ],
        compiler_params=pltpu.CompilerParams(
            collective_id=0, has_side_effects=True, vmem_limit_bytes=60 * 1024 * 1024
        ),
        cost_estimate=pl.CostEstimate(
            flops=4_000_000_000, bytes_accessed=4_000_000, transcendentals=1_600_000
        ),
    )(linear_query, linear_key, values, window_query, window_key, selections(lanes))


def solution(mesh):
    spec = P(("grp", "seq"), None)
    return jax.shard_map(
        on_device,
        mesh=mesh,
        in_specs=(spec,) * 5,
        out_specs=(spec, spec),
        check_vma=False,
    )
```

```python
import functools
import jax
import jax.numpy as jnp
import numpy as np
from jax import lax
from jax.experimental import pallas as pl
from jax.experimental.pallas import tpu as pltpu
from jax.sharding import PartitionSpec as P

FEAT = 16
WINDOW = 256
PAIRS = FEAT * (FEAT + 1) // 2
FEATS = 160
ONE_ROW = PAIRS + FEAT
CHUNKS = 4
MESH = pl.DeviceIdType.MESH
F32 = jnp.float32
BF16 = jnp.bfloat16


def selections(lanes):
    lower, upper = np.triu_indices(FEAT)
    left = np.zeros((FEATS, FEAT), np.float32)
    right = np.zeros((FEATS, FEAT), np.float32)
    right_query = np.zeros((FEATS, FEAT), np.float32)
    rows = np.arange(PAIRS)
    left[rows, lower] = 1.0
    right[rows, upper] = 1.0
    right_query[rows, upper] = np.where(lower == upper, 1.0, 2.0)
    left[PAIRS + np.arange(FEAT), np.arange(FEAT)] = 1.0
    stacked = np.stack([left, right, right_query])
    return jnp.asarray(np.tile(stacked, (1, 1, lanes // FEAT)), BF16)


def dot_t(a, b):
    return lax.dot_general(a, b, (((1,), (1,)), ((), ())), preferred_element_type=F32)


def dot(a, b):
    return jnp.dot(a, b, preferred_element_type=F32)


def kernel(
    pairs, rows, dim, heads,
    lq_ref, lk_ref, v_ref, wq_ref, wk_ref, sel_in,
    lin_ref, win_ref,
    sel_ref, lq2, lk2, v2, q2, k2, pv, pk, num, den, state, norm, state_in, norm_in, state_out, norm_out,
    lin_b, win_b, bias,
    xs, xr, zs, zr, ys, yr, cs, cr, rs, rr, ls,
):
    me = lax.axis_index("seq")
    pair = me // 2
    par = me % 2
    other = 1 - par
    partner = {"seq": pair * 2 + other}
    ahead = {"seq": jnp.minimum(me + 2, 2 * pairs - 1)}
    behind = {"seq": jnp.maximum(me - 2, 0)}
    has_next = pair < pairs - 1
    has_prev = pair > 0
    half_heads = heads // 2
    half = half_heads * dim
    width = half // CHUNKS
    per = width // dim
    lanes = half_heads * FEAT
    mine = pl.ds(pl.multiple_of(par * rows, rows), rows)
    theirs = pl.ds(pl.multiple_of(other * rows, rows), rows)

    def own_cols(c):
        return pl.ds(pl.multiple_of(par * half + c * width, width), width)

    def other_cols(c):
        return pl.ds(pl.multiple_of(other * half + c * width, width), width)

    def cols(c):
        return pl.ds(c * width if isinstance(c, int) else pl.multiple_of(c * width, width), width)

    barrier = pltpu.get_barrier_semaphore()
    pl.semaphore_signal(barrier, inc=1, device_id=partner, device_id_type=MESH)

    @pl.when(has_next)
    def _():
        pl.semaphore_signal(barrier, inc=1, device_id=ahead, device_id_type=MESH)

    @pl.when(has_prev)
    def _():
        pl.semaphore_signal(barrier, inc=1, device_id=behind, device_id_type=MESH)

    pl.semaphore_wait(barrier, 1 + jnp.minimum(pair, 1) + jnp.minimum(pairs - 1 - pair, 1))

    def remote(src, dst, send, recv, where):
        return pltpu.make_async_remote_copy(
            src_ref=src, dst_ref=dst, send_sem=send, recv_sem=recv,
            device_id=where, device_id_type=MESH,
        )

    small_other = pl.ds(pl.multiple_of(other * lanes, lanes), lanes)
    small_own = pl.ds(pl.multiple_of(par * lanes, lanes), lanes)

    def x_lk():
        return remote(lk_ref.at[:, small_other], lk2.at[mine, :], xs.at[0], xr.at[0], partner)

    def x_lq():
        return remote(lq_ref.at[:, small_other], lq2.at[mine, :], xs.at[1], xr.at[1], partner)

    def x_copy(src, dst, slot, c):
        at = 2 + slot * CHUNKS + c
        return remote(src.at[:, other_cols(c)], dst.at[mine, cols(c)], xs.at[at], xr.at[at], partner)

    def x_v(c):
        return x_copy(v_ref, v2, 0, c)

    def x_k(c):
        return x_copy(wk_ref, k2, 1, c)

    def x_q(c):
        return x_copy(wq_ref, q2, 2, c)

    def z_v(c):
        return remote(v_ref.at[:, own_cols(c)], pv.at[mine, cols(c)], zs.at[c], zr.at[c], ahead)

    def z_k(c):
        at = CHUNKS + c
        return remote(wk_ref.at[:, own_cols(c)], pk.at[mine, cols(c)], zs.at[at], zr.at[at], ahead)

    def y_v(c):
        return remote(v2.at[theirs, cols(c)], pv.at[theirs, cols(c)], ys.at[c], yr.at[c], ahead)

    def y_k(c):
        at = CHUNKS + c
        return remote(k2.at[theirs, cols(c)], pk.at[theirs, cols(c)], ys.at[at], yr.at[at], ahead)

    def c_state(c):
        return remote(state_out.at[c], state_in.at[c], cs.at[c], cr.at[c], ahead)

    def c_norm():
        return remote(norm_out, norm_in, cs.at[CHUNKS], cr.at[CHUNKS], ahead)

    def r_lin(c):
        return remote(lin_b.at[theirs, cols(c)], lin_ref.at[:, own_cols(c)], rs.at[c], rr.at[c], partner)

    def r_win(c):
        at = CHUNKS + c
        return remote(win_b.at[theirs, cols(c)], win_ref.at[:, own_cols(c)], rs.at[at], rr.at[at], partner)

    def local(src, dst, at):
        return pltpu.make_async_copy(src, dst, ls.at[at])

    def l_lin(c):
        return local(lin_b.at[mine, cols(c)], lin_ref.at[:, own_cols(c)], 6 + c)

    def l_win(c):
        return local(win_b.at[mine, cols(c)], win_ref.at[:, own_cols(c)], 6 + CHUNKS + c)

    x_lk().start()
    x_lq().start()
    for c in range(CHUNKS):
        x_v(c).start()

    @pl.when(has_next)
    def _():
        z_v(0).start()

    small = [
        local(sel_in, sel_ref, 0),
        local(lk_ref.at[:, small_own], lk2.at[mine, :], 1),
        local(lq_ref.at[:, small_own], lq2.at[mine, :], 2),
    ]
    all_own = pl.ds(pl.multiple_of(par * half, half), half)
    large = [
        local(v_ref.at[:, all_own], v2.at[mine, :], 3),
        local(wk_ref.at[:, all_own], k2.at[mine, :], 4),
        local(wq_ref.at[:, all_own], q2.at[mine, :], 5),
    ]
    for copy in small + large:
        copy.start()
    for c in range(CHUNKS):
        x_k(c).start()
    for c in range(CHUNKS):
        x_q(c).start()

    @pl.when(pair == 0)
    def _():
        pv[...] = jnp.zeros_like(pv)
        pk[...] = jnp.zeros_like(pk)
        state_in[...] = jnp.zeros_like(state_in)
        norm_in[...] = jnp.zeros_like(norm_in)

    norm[...] = jnp.zeros_like(norm)
    both = 2 * rows
    span = 3 * rows
    q_at = lax.broadcasted_iota(jnp.int32, (rows, span), 0)
    k_at = lax.broadcasted_iota(jnp.int32, (rows, span), 1)
    band = (k_at > q_at) & (k_at <= q_at + both)
    empty = jnp.where(pair == 0, 1, 0)
    for part in range(2):
        allowed = band & (k_at >= empty * (both - part * rows))
        bias[part] = jnp.where(allowed, 0.0, -1e30)
    for copy in small + large:
        copy.wait()
    x_lk().wait_recv()
    x_lq().wait_recv()

    ones = jnp.ones((both, dim), BF16)
    lane = lax.broadcasted_iota(jnp.int32, (both, lanes), 1) // FEAT
    row_at = lax.broadcasted_iota(jnp.int32, (both, both), 0)
    col_at = lax.broadcasted_iota(jnp.int32, (both, both), 1)
    causal = col_at <= row_at
    feat_row = lax.broadcasted_iota(jnp.int32, (FEATS, both), 0)
    row_left = jnp.where(feat_row == ONE_ROW, 1.0, 0.0)
    row_right = jnp.where((feat_row >= PAIRS) & (feat_row <= ONE_ROW), 1.0, 0.0)
    norm_lane = lax.broadcasted_iota(jnp.int32, (FEATS, 128), 1)

    def first(c, carry):
        x_v(c).wait_recv()
        for u in range(per):
            head = c * per + u
            at = pl.ds(pl.multiple_of(head * dim, dim), dim)
            chosen = lane == head
            keys = lk2[...]
            key_m = jnp.where(chosen, keys.astype(F32), 0.0).astype(BF16)
            query_m = jnp.where(chosen, lq2[...].astype(F32) * 0.25, 0.0).astype(BF16)
            values = jnp.concatenate([v2[:, at], ones], axis=1)
            feats = (dot_t(sel_ref[0], key_m) + row_left) * (dot_t(sel_ref[1], key_m) + row_right)
            summed = dot(feats.astype(BF16), values)
            state[head] = summed[:, :dim]
            norm[...] += jnp.where(norm_lane == head, summed[:, dim:], 0.0)
            a = dot_t(query_m, keys) + 1.0
            weight = jnp.where(causal, a * a + 1.0, 0.0).astype(BF16)
            mixed = dot(weight, values)
            num[:, at] = mixed[:, :dim]
            den[:, at] = mixed[:, dim:]

        @pl.when(has_prev)
        def _():
            c_state(c).wait_recv()

        @pl.when(has_next)
        def _():
            total = state_in[c].astype(F32) + state[pl.ds(c * per, per)]
            state_out[c] = total.astype(state_out.dtype)
            c_state(c).start()

        @pl.when(has_next & (c < CHUNKS - 1))
        def _():
            z_v(c + 1).start()

        return carry

    lax.fori_loop(0, CHUNKS, first, 0)

    @pl.when(has_prev)
    def _():
        c_norm().wait_recv()

    @pl.when(has_next)
    def _():
        norm_out[...] = norm_in[...] + norm[...]
        c_norm().start()

    for c in range(CHUNKS):
        x_k(c).wait_recv()

        @pl.when(has_next)
        def _():
            y_v(c).start()
            z_k(c).start()
            y_k(c).start()

    factor = dim ** -0.5 * 1.4426950408889634
    feat_lane = lax.broadcasted_iota(jnp.int32, (both, FEATS), 1)
    lane_left = jnp.where(feat_lane == ONE_ROW, 1.0, 0.0)
    lane_right = jnp.where((feat_lane >= PAIRS) & (feat_lane <= ONE_ROW), 2.0, 0.0)
    wide_ones = jnp.ones((span, dim), BF16)

    def second(c, carry):
        x_q(c).wait_recv()

        @pl.when(has_prev)
        def _():
            z_v(c).wait_recv()
            z_k(c).wait_recv()
            y_v(c).wait_recv()
            y_k(c).wait_recv()

        for u in range(per):
            head = c * per + u
            at = pl.ds(pl.multiple_of(head * dim, dim), dim)
            for part in range(2):
                begin = part * rows
                keys = jnp.concatenate([pk[begin:, at], k2[: begin + rows, at]], axis=0)
                values = jnp.concatenate([pv[begin:, at], v2[: begin + rows, at]], axis=0)
                scores = dot_t(q2[begin : begin + rows, at], keys) * factor + bias[part]
                largest = jnp.max(scores, axis=1, keepdims=True)
                weight = jnp.exp2(scores - largest).astype(BF16)
                mixed = dot(weight, jnp.concatenate([values, wide_ones], axis=1))
                win_b[begin : begin + rows, at] = (mixed[:, :dim] / mixed[:, dim:]).astype(BF16)

            query_m = jnp.where(lane == head, lq2[...].astype(F32) * 0.25, 0.0).astype(BF16)
            feats = (dot_t(query_m, sel_ref[0]) + lane_left) * (dot_t(query_m, sel_ref[2]) + lane_right)
            norm_col = jnp.sum(jnp.where(norm_lane == head, norm_in[...], 0.0), axis=1, keepdims=True)
            prior = jnp.concatenate(
                [state_in[c, u].astype(BF16), jnp.broadcast_to(norm_col, (FEATS, dim)).astype(BF16)], axis=1
            )
            added = dot(feats.astype(BF16), prior)
            linear = (num[:, at] + added[:, :dim]) / (den[:, at] + added[:, dim:])
            lin_b[:, at] = linear.astype(BF16)
        r_lin(c).start()
        r_win(c).start()
        l_lin(c).start()
        l_win(c).start()
        return carry

    lax.fori_loop(0, CHUNKS, second, 0)

    def last(c, carry):
        r_lin(c).wait_recv()
        r_win(c).wait_recv()
        l_lin(c).wait()
        l_win(c).wait()
        return carry

    lax.fori_loop(0, CHUNKS, last, 0)

    x_lk().wait_send()
    x_lq().wait_send()
    for c in range(CHUNKS):
        x_v(c).wait_send()
        x_k(c).wait_send()
        x_q(c).wait_send()
        r_lin(c).wait_send()
        r_win(c).wait_send()

    @pl.when(has_next)
    def _():
        c_norm().wait_send()
        for c in range(CHUNKS):
            z_v(c).wait_send()
            z_k(c).wait_send()
            y_v(c).wait_send()
            y_k(c).wait_send()
            c_state(c).wait_send()


def on_device(linear_query, linear_key, values, window_query, window_key):
    rows, width = values.shape
    heads = linear_query.shape[1] // FEAT
    dim = width // heads
    pairs = lax.axis_size("seq") // 2
    half_heads = heads // 2
    half = width // 2
    lanes = half_heads * FEAT
    both = 2 * rows
    per = half_heads // CHUNKS
    state_type = BF16 if pairs <= 8 else F32
    dma = pltpu.SemaphoreType.DMA
    linear, window = pl.pallas_call(
        functools.partial(kernel, pairs, rows, dim, heads),
        out_shape=(
            jax.ShapeDtypeStruct((rows, width), BF16),
            jax.ShapeDtypeStruct((rows, width), BF16),
        ),
        in_specs=[pl.BlockSpec(memory_space=pl.ANY)] * 6,
        out_specs=(pl.BlockSpec(memory_space=pl.ANY),) * 2,
        scratch_shapes=[
            pltpu.VMEM((3, FEATS, lanes), BF16),
            pltpu.VMEM((both, lanes), BF16),
            pltpu.VMEM((both, lanes), BF16),
            pltpu.VMEM((both, half), BF16),
            pltpu.VMEM((both, half), BF16),
            pltpu.VMEM((both, half), BF16),
            pltpu.VMEM((both, half), BF16),
            pltpu.VMEM((both, half), BF16),
            pltpu.VMEM((both, half), F32),
            pltpu.VMEM((both, half), F32),
            pltpu.VMEM((half_heads, FEATS, dim), F32),
            pltpu.VMEM((FEATS, 128), F32),
            pltpu.VMEM((CHUNKS, per, FEATS, dim), state_type),
            pltpu.VMEM((FEATS, 128), F32),
            pltpu.VMEM((CHUNKS, per, FEATS, dim), state_type),
            pltpu.VMEM((FEATS, 128), F32),
            pltpu.VMEM((both, half), BF16),
            pltpu.VMEM((both, half), BF16),
            pltpu.VMEM((2, rows, 3 * rows), F32),
            dma((2 + 3 * CHUNKS,)),
            dma((2 + 3 * CHUNKS,)),
            dma((2 * CHUNKS,)),
            dma((2 * CHUNKS,)),
            dma((2 * CHUNKS,)),
            dma((2 * CHUNKS,)),
            dma((CHUNKS + 1,)),
            dma((CHUNKS + 1,)),
            dma((2 * CHUNKS,)),
            dma((2 * CHUNKS,)),
            dma((6 + 2 * CHUNKS,)),
        ],
        compiler_params=pltpu.CompilerParams(
            collective_id=0, has_side_effects=True, vmem_limit_bytes=60 * 1024 * 1024
        ),
        cost_estimate=pl.CostEstimate(
            flops=4_000_000_000, bytes_accessed=4_000_000, transcendentals=1_600_000
        ),
    )(linear_query, linear_key, values, window_query, window_key, selections(lanes))
    return linear.astype(F32), window


def solution(mesh):
    spec = P(("grp", "seq"), None)
    return jax.shard_map(
        on_device,
        mesh=mesh,
        in_specs=(spec,) * 5,
        out_specs=(spec, spec),
        check_vma=False,
    )
```

```python
import functools
import jax
import jax.numpy as jnp
import numpy as np
from jax import lax
from jax.experimental import pallas as pl
from jax.experimental.pallas import tpu as pltpu
from jax.sharding import PartitionSpec as P

FEAT = 16
WINDOW = 256
PAIRS = FEAT * (FEAT + 1) // 2
FEATS = 160
ONE_ROW = PAIRS + FEAT
CHUNKS = 4
MESH = pl.DeviceIdType.MESH
F32 = jnp.float32
BF16 = jnp.bfloat16


def selections(lanes):
    lower, upper = np.triu_indices(FEAT)
    left = np.zeros((FEATS, FEAT), np.float32)
    right = np.zeros((FEATS, FEAT), np.float32)
    right_query = np.zeros((FEATS, FEAT), np.float32)
    rows = np.arange(PAIRS)
    left[rows, lower] = 1.0
    right[rows, upper] = 1.0
    right_query[rows, upper] = np.where(lower == upper, 1.0, 2.0)
    left[PAIRS + np.arange(FEAT), np.arange(FEAT)] = 1.0
    stacked = np.stack([left, right, right_query])
    return jnp.asarray(np.tile(stacked, (1, 1, lanes // FEAT)), BF16)


def dot_t(a, b):
    return lax.dot_general(a, b, (((1,), (1,)), ((), ())), preferred_element_type=F32)


def dot(a, b):
    return jnp.dot(a, b, preferred_element_type=F32)


def kernel(
    pairs, rows, dim, heads,
    lq_ref, lk_ref, v_ref, wq_ref, wk_ref, sel_in,
    lin_ref, win_ref,
    sel_ref, lqs, lks, vs, qs, ks, qf, lq2, lk2, v2, q2, k2, pv, pk, num, den, state, norm, state_in, norm_in, state_out, norm_out,
    lin_b, win_b, bias,
    xs, xr, zs, zr, ys, yr, cs, cr, rs, rr, ls,
):
    me = lax.axis_index("seq")
    pair = me // 2
    par = me % 2
    other = 1 - par
    partner = {"seq": pair * 2 + other}
    ahead = {"seq": jnp.minimum(me + 2, 2 * pairs - 1)}
    behind = {"seq": jnp.maximum(me - 2, 0)}
    has_next = pair < pairs - 1
    has_prev = pair > 0
    half_heads = heads // 2
    half = half_heads * dim
    width = half // CHUNKS
    per = width // dim
    lanes = half_heads * FEAT
    mine = pl.ds(pl.multiple_of(par * rows, rows), rows)
    theirs = pl.ds(pl.multiple_of(other * rows, rows), rows)

    def own_cols(c):
        return pl.ds(pl.multiple_of(par * half + c * width, width), width)

    def cols(c):
        return pl.ds(c * width if isinstance(c, int) else pl.multiple_of(c * width, width), width)

    small_other = pl.ds(pl.multiple_of(other * lanes, lanes), lanes)
    small_own = pl.ds(pl.multiple_of(par * lanes, lanes), lanes)
    all_own = pl.ds(pl.multiple_of(par * half, half), half)
    all_other = pl.ds(pl.multiple_of(other * half, half), half)

    def local(src, dst, at):
        return pltpu.make_async_copy(src, dst, ls.at[at])

    fetched = [
        local(lk_ref.at[:, small_other], lks, 0),
        local(lq_ref.at[:, small_other], lqs, 1),
        local(v_ref.at[:, all_other], vs, 2),
        local(v_ref.at[:, all_own], v2.at[mine, :], 3),
        local(wk_ref.at[:, all_other], ks, 4),
        local(wk_ref.at[:, all_own], k2.at[mine, :], 5),
        local(wq_ref.at[:, all_other], qs, 6),
        local(wq_ref.at[:, all_own], q2.at[mine, :], 7),
        local(lk_ref.at[:, small_own], lk2.at[mine, :], 8),
        local(lq_ref.at[:, small_own], lq2.at[mine, :], 9),
        local(sel_in, sel_ref, 10),
    ]
    for copy in fetched:
        copy.start()

    barrier = pltpu.get_barrier_semaphore()
    pl.semaphore_signal(barrier, inc=1, device_id=partner, device_id_type=MESH)

    @pl.when(has_next)
    def _():
        pl.semaphore_signal(barrier, inc=1, device_id=ahead, device_id_type=MESH)

    @pl.when(has_prev)
    def _():
        pl.semaphore_signal(barrier, inc=1, device_id=behind, device_id_type=MESH)

    pl.semaphore_wait(barrier, 1 + jnp.minimum(pair, 1) + jnp.minimum(pairs - 1 - pair, 1))

    def remote(src, dst, send, recv, where):
        return pltpu.make_async_remote_copy(
            src_ref=src, dst_ref=dst, send_sem=send, recv_sem=recv,
            device_id=where, device_id_type=MESH,
        )

    def x_lk():
        return remote(lks, lk2.at[mine, :], xs.at[0], xr.at[0], partner)

    def x_lq():
        return remote(lqs, lq2.at[mine, :], xs.at[1], xr.at[1], partner)

    def x_copy(src, dst, slot, c):
        at = 2 + slot * CHUNKS + c
        return remote(src.at[:, cols(c)], dst.at[mine, cols(c)], xs.at[at], xr.at[at], partner)

    def x_v(c):
        return x_copy(vs, v2, 0, c)

    def x_k(c):
        return x_copy(ks, k2, 1, c)

    def x_q(c):
        return x_copy(qs, q2, 2, c)

    def z_v(c):
        return remote(v2.at[mine, cols(c)], pv.at[mine, cols(c)], zs.at[c], zr.at[c], ahead)

    def z_k(c):
        at = CHUNKS + c
        return remote(k2.at[mine, cols(c)], pk.at[mine, cols(c)], zs.at[at], zr.at[at], ahead)

    def y_v(c):
        return remote(v2.at[theirs, cols(c)], pv.at[theirs, cols(c)], ys.at[c], yr.at[c], ahead)

    def y_k(c):
        at = CHUNKS + c
        return remote(k2.at[theirs, cols(c)], pk.at[theirs, cols(c)], ys.at[at], yr.at[at], ahead)

    def c_state(c):
        return remote(state_out.at[c], state_in.at[c], cs.at[c], cr.at[c], ahead)

    def c_norm():
        return remote(norm_out, norm_in, cs.at[CHUNKS], cr.at[CHUNKS], ahead)

    def r_lin(c):
        return remote(lin_b.at[theirs, cols(c)], lin_ref.at[:, own_cols(c)], rs.at[c], rr.at[c], partner)

    def r_win(c):
        at = CHUNKS + c
        return remote(win_b.at[theirs, cols(c)], win_ref.at[:, own_cols(c)], rs.at[at], rr.at[at], partner)

    def l_lin(c):
        return local(lin_b.at[mine, cols(c)], lin_ref.at[:, own_cols(c)], 11 + c)

    def l_win(c):
        return local(win_b.at[mine, cols(c)], win_ref.at[:, own_cols(c)], 11 + CHUNKS + c)

    for copy in fetched:
        copy.wait()
    x_lk().start()
    x_lq().start()
    for c in range(CHUNKS):
        x_v(c).start()

    @pl.when(has_next)
    def _():
        z_v(0).start()

    for c in range(CHUNKS):
        x_k(c).start()
    for c in range(CHUNKS):
        x_q(c).start()

    @pl.when(pair == 0)
    def _():
        pv[...] = jnp.zeros_like(pv)
        pk[...] = jnp.zeros_like(pk)
        state_in[...] = jnp.zeros_like(state_in)
        norm_in[...] = jnp.zeros_like(norm_in)

    norm[...] = jnp.zeros_like(norm)
    both = 2 * rows
    span = 3 * rows
    q_at = lax.broadcasted_iota(jnp.int32, (rows, span), 0)
    k_at = lax.broadcasted_iota(jnp.int32, (rows, span), 1)
    band = (k_at > q_at) & (k_at <= q_at + both)
    empty = jnp.where(pair == 0, 1, 0)
    for part in range(2):
        allowed = band & (k_at >= empty * (both - part * rows))
        bias[part] = jnp.where(allowed, 0.0, -1e30)
    x_lk().wait_recv()
    x_lq().wait_recv()

    ones = jnp.ones((both, dim), BF16)
    lane = lax.broadcasted_iota(jnp.int32, (both, lanes), 1) // FEAT
    row_at = lax.broadcasted_iota(jnp.int32, (both, both), 0)
    col_at = lax.broadcasted_iota(jnp.int32, (both, both), 1)
    causal = col_at <= row_at
    feat_row = lax.broadcasted_iota(jnp.int32, (FEATS, both), 0)
    row_left = jnp.where(feat_row == ONE_ROW, 1.0, 0.0)
    row_right = jnp.where((feat_row >= PAIRS) & (feat_row <= ONE_ROW), 1.0, 0.0)
    norm_lane = lax.broadcasted_iota(jnp.int32, (FEATS, 128), 1)

    feat_lane = lax.broadcasted_iota(jnp.int32, (both, FEATS), 1)
    lane_left = jnp.where(feat_lane == ONE_ROW, 1.0, 0.0)
    lane_right = jnp.where((feat_lane >= PAIRS) & (feat_lane <= ONE_ROW), 2.0, 0.0)

    def first(c, carry):
        x_v(c).wait_recv()

        @pl.when(has_next)
        def _():
            y_v(c).start()

        todo = range(per)
        keys = lk2[...]
        head = [c * per + u for u in todo]
        at = [pl.ds(pl.multiple_of(head[u] * dim, dim), dim) for u in todo]
        key_m = [jnp.where(lane == head[u], keys.astype(F32), 0.0).astype(BF16) for u in todo]
        query_m = [jnp.where(lane == head[u], lq2[...].astype(F32) * 0.25, 0.0).astype(BF16) for u in todo]
        values = [jnp.concatenate([v2[:, at[u]], ones], axis=1) for u in todo]
        left = [dot_t(sel_ref[0], key_m[u]) for u in todo]
        right = [dot_t(sel_ref[1], key_m[u]) for u in todo]
        a = [dot_t(query_m[u], keys) + 1.0 for u in todo]
        feats = [((left[u] + row_left) * (right[u] + row_right)).astype(BF16) for u in todo]
        summed = [dot(feats[u], values[u]) for u in todo]
        weight = [jnp.where(causal, a[u] * a[u] + 1.0, 0.0).astype(BF16) for u in todo]
        mixed = [dot(weight[u], values[u]) for u in todo]
        for u in todo:
            state[head[u]] = summed[u][:, :dim]
            norm[...] += jnp.where(norm_lane == head[u], summed[u][:, dim:], 0.0)

        @pl.when(has_next & (pair == 0))
        def _():
            for u in todo:
                state_out[c, u] = summed[u][:, :dim].astype(state_out.dtype)
            c_state(c).start()

        @pl.when(has_next & (c < CHUNKS - 1))
        def _():
            z_v(c + 1).start()

        left = [dot_t(query_m[u], sel_ref[0]) for u in todo]
        right = [dot_t(query_m[u], sel_ref[2]) for u in todo]
        for u in todo:
            num[:, at[u]] = mixed[u][:, :dim]
            den[:, at[u]] = mixed[u][:, dim:]
            qf[head[u]] = ((left[u] + lane_left) * (right[u] + lane_right)).astype(BF16)
        return carry

    lax.fori_loop(0, CHUNKS, first, 0)

    @pl.when(has_prev)
    def _():
        c_norm().wait_recv()

    @pl.when(has_next)
    def _():
        norm_out[...] = norm_in[...] + norm[...]
        c_norm().start()

    def chain(c):
        @pl.when(has_prev)
        def _():
            c_state(c).wait_recv()

        @pl.when(has_prev & has_next)
        def _():
            total = state_in[c].astype(F32) + state[c * per : (c + 1) * per]
            state_out[c] = total.astype(state_out.dtype)
            c_state(c).start()

    def bulk(c):
        x_k(c).wait_recv()

        @pl.when(has_next)
        def _():
            z_k(c).start()
            y_k(c).start()

    early = CHUNKS // 2
    for c in range(early):
        chain(c)

    @pl.when(pair < 2)
    def _():
        for c in range(early, CHUNKS):
            chain(c)

    for c in range(early):
        bulk(c)

    @pl.when(pair < 2)
    def _():
        for c in range(early, CHUNKS):
            bulk(c)

    factor = dim ** -0.5 * 1.4426950408889634
    wide_ones = jnp.ones((span, dim), BF16)

    def second(c, carry):
        @pl.when((c == 1) & (pair >= 2))
        def _():
            for late in range(early, CHUNKS):
                chain(late)
            for late in range(early, CHUNKS):
                bulk(late)

        x_q(c).wait_recv()

        @pl.when(has_prev)
        def _():
            z_v(c).wait_recv()
            z_k(c).wait_recv()
            y_v(c).wait_recv()
            y_k(c).wait_recv()

        todo = range(per)
        head = [c * per + u for u in todo]
        at = [pl.ds(pl.multiple_of(head[u] * dim, dim), dim) for u in todo]
        both_parts = [(u, part, part * rows) for u in todo for part in range(2)]
        scores = []
        for u, part, begin in both_parts:
            keys = jnp.concatenate([pk[begin:, at[u]], k2[: begin + rows, at[u]]], axis=0)
            scores.append(dot_t(q2[begin : begin + rows, at[u]], keys))
        scores = [scores[i] * factor + bias[part] for i, (u, part, begin) in enumerate(both_parts)]
        largest = [jnp.max(score, axis=1, keepdims=True) for score in scores]
        weights = [jnp.exp2(scores[i] - largest[i]).astype(BF16) for i in range(len(scores))]
        mixed = []
        for i, (u, part, begin) in enumerate(both_parts):
            values = jnp.concatenate([pv[begin:, at[u]], v2[: begin + rows, at[u]]], axis=0)
            mixed.append(dot(weights[i], jnp.concatenate([values, wide_ones], axis=1)))
        added = []
        for u in todo:
            norm_col = jnp.sum(jnp.where(norm_lane == head[u], norm_in[...], 0.0), axis=1, keepdims=True)
            prior = jnp.concatenate(
                [state_in[c, u].astype(BF16), jnp.broadcast_to(norm_col, (FEATS, dim)).astype(BF16)], axis=1
            )
            added.append(dot(qf[head[u]], prior))
        for i, (u, part, begin) in enumerate(both_parts):
            win_b[begin : begin + rows, at[u]] = (mixed[i][:, :dim] / mixed[i][:, dim:]).astype(BF16)
        for u in todo:
            linear = (num[:, at[u]] + added[u][:, :dim]) / (den[:, at[u]] + added[u][:, dim:])
            lin_b[:, at[u]] = linear.astype(BF16)
        r_lin(c).start()
        r_win(c).start()
        l_lin(c).start()
        l_win(c).start()
        return carry

    lax.fori_loop(0, CHUNKS, second, 0)

    def last(c, carry):
        r_lin(c).wait_recv()
        r_win(c).wait_recv()
        l_lin(c).wait()
        l_win(c).wait()
        return carry

    lax.fori_loop(0, CHUNKS, last, 0)

    x_lk().wait_send()
    x_lq().wait_send()
    for c in range(CHUNKS):
        x_v(c).wait_send()
        x_k(c).wait_send()
        x_q(c).wait_send()
        r_lin(c).wait_send()
        r_win(c).wait_send()

    @pl.when(has_next)
    def _():
        c_norm().wait_send()
        for c in range(CHUNKS):
            z_v(c).wait_send()
            z_k(c).wait_send()
            y_v(c).wait_send()
            y_k(c).wait_send()
            c_state(c).wait_send()


def on_device(linear_query, linear_key, values, window_query, window_key):
    rows, width = values.shape
    heads = linear_query.shape[1] // FEAT
    dim = width // heads
    pairs = lax.axis_size("seq") // 2
    half_heads = heads // 2
    half = width // 2
    lanes = half_heads * FEAT
    both = 2 * rows
    per = half_heads // CHUNKS
    state_type = BF16 if pairs <= 8 else F32
    dma = pltpu.SemaphoreType.DMA
    linear, window = pl.pallas_call(
        functools.partial(kernel, pairs, rows, dim, heads),
        out_shape=(
            jax.ShapeDtypeStruct((rows, width), BF16),
            jax.ShapeDtypeStruct((rows, width), BF16),
        ),
        in_specs=[pl.BlockSpec(memory_space=pl.ANY)] * 6,
        out_specs=(pl.BlockSpec(memory_space=pl.ANY),) * 2,
        scratch_shapes=[
            pltpu.VMEM((3, FEATS, lanes), BF16),
            pltpu.VMEM((rows, lanes), BF16),
            pltpu.VMEM((rows, lanes), BF16),
            pltpu.VMEM((rows, half), BF16),
            pltpu.VMEM((rows, half), BF16),
            pltpu.VMEM((rows, half), BF16),
            pltpu.VMEM((half_heads, both, FEATS), BF16),
            pltpu.VMEM((both, lanes), BF16),
            pltpu.VMEM((both, lanes), BF16),
            pltpu.VMEM((both, half), BF16),
            pltpu.VMEM((both, half), BF16),
            pltpu.VMEM((both, half), BF16),
            pltpu.VMEM((both, half), BF16),
            pltpu.VMEM((both, half), BF16),
            pltpu.VMEM((both, half), F32),
            pltpu.VMEM((both, half), F32),
            pltpu.VMEM((half_heads, FEATS, dim), F32),
            pltpu.VMEM((FEATS, 128), F32),
            pltpu.VMEM((CHUNKS, per, FEATS, dim), state_type),
            pltpu.VMEM((FEATS, 128), F32),
            pltpu.VMEM((CHUNKS, per, FEATS, dim), state_type),
            pltpu.VMEM((FEATS, 128), F32),
            pltpu.VMEM((both, half), BF16),
            pltpu.VMEM((both, half), BF16),
            pltpu.VMEM((2, rows, 3 * rows), F32),
            dma((2 + 3 * CHUNKS,)),
            dma((2 + 3 * CHUNKS,)),
            dma((2 * CHUNKS,)),
            dma((2 * CHUNKS,)),
            dma((2 * CHUNKS,)),
            dma((2 * CHUNKS,)),
            dma((CHUNKS + 1,)),
            dma((CHUNKS + 1,)),
            dma((2 * CHUNKS,)),
            dma((2 * CHUNKS,)),
            dma((11 + 2 * CHUNKS,)),
        ],
        compiler_params=pltpu.CompilerParams(
            collective_id=0, has_side_effects=True, vmem_limit_bytes=60 * 1024 * 1024
        ),
        cost_estimate=pl.CostEstimate(
            flops=4_000_000_000, bytes_accessed=4_000_000, transcendentals=1_600_000
        ),
    )(linear_query, linear_key, values, window_query, window_key, selections(lanes))
    return linear.astype(F32), window


def solution(mesh):
    spec = P(("grp", "seq"), None)
    return jax.shard_map(
        on_device,
        mesh=mesh,
        in_specs=(spec,) * 5,
        out_specs=(spec, spec),
        check_vma=False,
    )
```

```python
import functools
import jax
import jax.numpy as jnp
import numpy as np
from jax import lax
from jax.experimental import pallas as pl
from jax.experimental.pallas import tpu as pltpu
from jax.sharding import PartitionSpec as P

FEAT = 16
WINDOW = 256
PAIRS = FEAT * (FEAT + 1) // 2
FEATS = 160
ONE_ROW = PAIRS + FEAT
CHUNKS = 4
MESH = pl.DeviceIdType.MESH
F32 = jnp.float32
BF16 = jnp.bfloat16


def selections(lanes):
    lower, upper = np.triu_indices(FEAT)
    left = np.zeros((FEATS, FEAT), np.float32)
    right = np.zeros((FEATS, FEAT), np.float32)
    right_query = np.zeros((FEATS, FEAT), np.float32)
    rows = np.arange(PAIRS)
    left[rows, lower] = 1.0
    right[rows, upper] = 1.0
    right_query[rows, upper] = np.where(lower == upper, 1.0, 2.0)
    left[PAIRS + np.arange(FEAT), np.arange(FEAT)] = 1.0
    stacked = np.stack([left, right, right_query])
    return jnp.asarray(np.tile(stacked, (1, 1, lanes // FEAT)), BF16)


def dot_t(a, b):
    return lax.dot_general(a, b, (((1,), (1,)), ((), ())), preferred_element_type=F32)


def dot(a, b):
    return jnp.dot(a, b, preferred_element_type=F32)


def kernel(
    pairs, rows, dim, heads,
    lq_ref, lk_ref, v_ref, wq_ref, wk_ref, sel_in,
    lin_ref, win_ref,
    sel_ref, lqs, lks, vs, qs, ks, qf, lq2, lk2, v2, q2, k2, qn, part_out, part_in, log_out, log_in, own, own_log, num, den, state, norm, state_in, norm_in, state_out, norm_out,
    lin_b, win_b, bias,
    xs, xr, zs, zr, ps, pr, cs, cr, rs, rr, ls,
):
    me = lax.axis_index("seq")
    pair = me // 2
    par = me % 2
    other = 1 - par
    partner = {"seq": pair * 2 + other}
    ahead = {"seq": jnp.minimum(me + 2, 2 * pairs - 1)}
    behind = {"seq": jnp.maximum(me - 2, 0)}
    has_next = pair < pairs - 1
    has_prev = pair > 0
    half_heads = heads // 2
    half = half_heads * dim
    width = half // CHUNKS
    per = width // dim
    lanes = half_heads * FEAT
    mine = pl.ds(pl.multiple_of(par * rows, rows), rows)
    theirs = pl.ds(pl.multiple_of(other * rows, rows), rows)

    def own_cols(c):
        return pl.ds(pl.multiple_of(par * half + c * width, width), width)

    def cols(c):
        return pl.ds(c * width if isinstance(c, int) else pl.multiple_of(c * width, width), width)

    small_other = pl.ds(pl.multiple_of(other * lanes, lanes), lanes)
    small_own = pl.ds(pl.multiple_of(par * lanes, lanes), lanes)
    all_own = pl.ds(pl.multiple_of(par * half, half), half)
    all_other = pl.ds(pl.multiple_of(other * half, half), half)

    def local(src, dst, at):
        return pltpu.make_async_copy(src, dst, ls.at[at])

    fetched = [
        local(lk_ref.at[:, small_other], lks, 0),
        local(lq_ref.at[:, small_other], lqs, 1),
        local(v_ref.at[:, all_other], vs, 2),
        local(v_ref.at[:, all_own], v2.at[mine, :], 3),
        local(wk_ref.at[:, all_other], ks, 4),
        local(wk_ref.at[:, all_own], k2.at[mine, :], 5),
        local(wq_ref.at[:, all_other], qs, 6),
        local(wq_ref.at[:, all_own], q2.at[mine, :], 7),
        local(lk_ref.at[:, small_own], lk2.at[mine, :], 8),
        local(lq_ref.at[:, small_own], lq2.at[mine, :], 9),
        local(sel_in, sel_ref, 10),
    ]
    for copy in fetched:
        copy.start()

    barrier = pltpu.get_barrier_semaphore()
    pl.semaphore_signal(barrier, inc=1, device_id=partner, device_id_type=MESH)

    @pl.when(has_next)
    def _():
        pl.semaphore_signal(barrier, inc=1, device_id=ahead, device_id_type=MESH)

    @pl.when(has_prev)
    def _():
        pl.semaphore_signal(barrier, inc=1, device_id=behind, device_id_type=MESH)

    pl.semaphore_wait(barrier, 1 + jnp.minimum(pair, 1) + jnp.minimum(pairs - 1 - pair, 1))

    def remote(src, dst, send, recv, where):
        return pltpu.make_async_remote_copy(
            src_ref=src, dst_ref=dst, send_sem=send, recv_sem=recv,
            device_id=where, device_id_type=MESH,
        )

    def x_lk():
        return remote(lks, lk2.at[mine, :], xs.at[0], xr.at[0], partner)

    def x_lq():
        return remote(lqs, lq2.at[mine, :], xs.at[1], xr.at[1], partner)

    def x_copy(src, dst, slot, c):
        at = 2 + slot * CHUNKS + c
        return remote(src.at[:, cols(c)], dst.at[mine, cols(c)], xs.at[at], xr.at[at], partner)

    def x_v(c):
        return x_copy(vs, v2, 0, c)

    def x_k(c):
        return x_copy(ks, k2, 1, c)

    def x_q(c):
        return x_copy(qs, q2, 2, c)

    def z_q(c):
        return remote(q2.at[mine, cols(c)], qn.at[mine, cols(c)], zs.at[c], zr.at[c], behind)

    def y_q(c):
        at = CHUNKS + c
        return remote(q2.at[theirs, cols(c)], qn.at[theirs, cols(c)], zs.at[at], zr.at[at], behind)

    def p_out(c):
        return remote(part_out.at[:, cols(c)], part_in.at[:, cols(c)], ps.at[c], pr.at[c], ahead)

    def p_log(c):
        at = CHUNKS + c
        return remote(log_out.at[c], log_in.at[c], ps.at[at], pr.at[at], ahead)

    def c_state(c):
        return remote(state_out.at[c], state_in.at[c], cs.at[c], cr.at[c], ahead)

    def c_norm():
        return remote(norm_out, norm_in, cs.at[CHUNKS], cr.at[CHUNKS], ahead)

    def r_lin(c):
        return remote(lin_b.at[theirs, cols(c)], lin_ref.at[:, own_cols(c)], rs.at[c], rr.at[c], partner)

    def r_win(c):
        at = CHUNKS + c
        return remote(win_b.at[theirs, cols(c)], win_ref.at[:, own_cols(c)], rs.at[at], rr.at[at], partner)

    def l_lin(c):
        return local(lin_b.at[mine, cols(c)], lin_ref.at[:, own_cols(c)], 11 + c)

    def l_win(c):
        return local(win_b.at[mine, cols(c)], win_ref.at[:, own_cols(c)], 11 + CHUNKS + c)

    for copy in fetched:
        copy.wait()
    x_lk().start()
    x_lq().start()
    for c in range(CHUNKS):
        x_v(c).start()
    for c in range(CHUNKS):
        x_q(c).start()
        x_k(c).start()

        @pl.when(has_prev)
        def _():
            z_q(c).start()

    @pl.when(pair == 0)
    def _():
        part_in[...] = jnp.zeros_like(part_in)
        log_in[...] = jnp.full_like(log_in, -1e30)
        state_in[...] = jnp.zeros_like(state_in)
        norm_in[...] = jnp.zeros_like(norm_in)

    norm[...] = jnp.zeros_like(norm)
    both = 2 * rows
    row_at = lax.broadcasted_iota(jnp.int32, (both, both), 0)
    col_at = lax.broadcasted_iota(jnp.int32, (both, both), 1)
    causal = col_at <= row_at
    bias[0] = jnp.where(causal, 0.0, -1e30)
    bias[1] = jnp.where(causal, -1e30, 0.0)
    x_lk().wait_recv()
    x_lq().wait_recv()

    ones = jnp.ones((both, dim), BF16)
    lane = lax.broadcasted_iota(jnp.int32, (both, lanes), 1) // FEAT
    feat_row = lax.broadcasted_iota(jnp.int32, (FEATS, both), 0)
    row_left = jnp.where(feat_row == ONE_ROW, 1.0, 0.0)
    row_right = jnp.where((feat_row >= PAIRS) & (feat_row <= ONE_ROW), 1.0, 0.0)
    norm_lane = lax.broadcasted_iota(jnp.int32, (FEATS, 128), 1)

    feat_lane = lax.broadcasted_iota(jnp.int32, (both, FEATS), 1)
    lane_left = jnp.where(feat_lane == ONE_ROW, 1.0, 0.0)
    lane_right = jnp.where((feat_lane >= PAIRS) & (feat_lane <= ONE_ROW), 2.0, 0.0)

    def first(c, carry):
        x_v(c).wait_recv()
        todo = range(per)
        keys = lk2[...]
        head = [c * per + u for u in todo]
        at = [pl.ds(pl.multiple_of(head[u] * dim, dim), dim) for u in todo]
        key_m = [jnp.where(lane == head[u], keys.astype(F32), 0.0).astype(BF16) for u in todo]
        query_m = [jnp.where(lane == head[u], lq2[...].astype(F32) * 0.25, 0.0).astype(BF16) for u in todo]
        values = [jnp.concatenate([v2[:, at[u]], ones], axis=1) for u in todo]
        left = [dot_t(sel_ref[0], key_m[u]) for u in todo]
        right = [dot_t(sel_ref[1], key_m[u]) for u in todo]
        a = [dot_t(query_m[u], keys) + 1.0 for u in todo]
        feats = [((left[u] + row_left) * (right[u] + row_right)).astype(BF16) for u in todo]
        summed = [dot(feats[u], values[u]) for u in todo]
        weight = [jnp.where(causal, a[u] * a[u] + 1.0, 0.0).astype(BF16) for u in todo]
        mixed = [dot(weight[u], values[u]) for u in todo]
        for u in todo:
            state[head[u]] = summed[u][:, :dim]
            norm[...] += jnp.where(norm_lane == head[u], summed[u][:, dim:], 0.0)

        @pl.when(has_next & (pair == 0))
        def _():
            for u in todo:
                state_out[c, u] = summed[u][:, :dim].astype(state_out.dtype)
            c_state(c).start()

        left = [dot_t(query_m[u], sel_ref[0]) for u in todo]
        right = [dot_t(query_m[u], sel_ref[2]) for u in todo]
        for u in todo:
            num[:, at[u]] = mixed[u][:, :dim]
            den[:, at[u]] = mixed[u][:, dim:]
            qf[head[u]] = ((left[u] + lane_left) * (right[u] + lane_right)).astype(BF16)
        return carry

    lax.fori_loop(0, CHUNKS, first, 0)

    @pl.when(has_prev)
    def _():
        c_norm().wait_recv()

    @pl.when(has_next)
    def _():
        norm_out[...] = norm_in[...] + norm[...]
        c_norm().start()

    def chain(c):
        @pl.when(has_prev)
        def _():
            c_state(c).wait_recv()

        @pl.when(has_prev & has_next)
        def _():
            total = state_in[c].astype(F32) + state[pl.ds(c * per, per)]
            state_out[c] = total.astype(state_out.dtype)
            c_state(c).start()

    factor = dim ** -0.5 * 1.4426950408889634
    head_lane = lax.broadcasted_iota(jnp.int32, (both, 128), 1)
    todo = range(per)

    def heads_at(c):
        head = [c * per + u for u in todo]
        return head, [pl.ds(pl.multiple_of(head[u] * dim, dim), dim) for u in todo]

    def attend(queries, at, which):
        scores = [dot_t(queries[:, at[u]], k2[:, at[u]]) for u in todo]
        scores = [scores[u] * factor + bias[which] for u in todo]
        largest = [jnp.max(scores[u], axis=1, keepdims=True) for u in todo]
        weights = [jnp.exp2(scores[u] - largest[u]).astype(BF16) for u in todo]
        mixed = [dot(weights[u], jnp.concatenate([v2[:, at[u]], ones], axis=1)) for u in todo]
        outs = [mixed[u][:, :dim] / mixed[u][:, dim:] for u in todo]
        return outs, [largest[u] + jnp.log2(mixed[u][:, dim:]) for u in todo]

    def second(c, carry):
        x_q(c).wait_recv()

        @pl.when(has_prev)
        def _():
            y_q(c).start()

        x_k(c).wait_recv()
        chain(c)
        head, at = heads_at(c)
        outs, logs = attend(q2, at, 0)
        added = []
        for u in todo:
            norm_col = jnp.sum(jnp.where(norm_lane == head[u], norm_in[...], 0.0), axis=1, keepdims=True)
            prior = jnp.concatenate(
                [state_in[c, u].astype(BF16), jnp.broadcast_to(norm_col, (FEATS, dim)).astype(BF16)], axis=1
            )
            added.append(dot(qf[head[u]], prior))
        for u in todo:
            own[:, at[u]] = outs[u]
            own_log[:, at[u]] = logs[u]
            linear = (num[:, at[u]] + added[u][:, :dim]) / (den[:, at[u]] + added[u][:, dim:])
            lin_b[:, at[u]] = linear.astype(BF16)
        r_lin(c).start()
        l_lin(c).start()

        @pl.when(has_next)
        def _():
            z_q(c).wait_recv()
            y_q(c).wait_recv()
            outs, logs = attend(qn, at, 1)
            packed = jnp.zeros((both, 128), F32)
            for u in todo:
                part_out[:, at[u]] = outs[u].astype(BF16)
                packed = jnp.where(head_lane == u, logs[u], packed)
            log_out[c] = jnp.transpose(packed)[:8]
            p_out(c).start()
            p_log(c).start()

        return carry

    lax.fori_loop(0, CHUNKS, second, 0)

    def third(c, carry):
        @pl.when(has_prev)
        def _():
            p_out(c).wait_recv()
            p_log(c).wait_recv()

        head, at = heads_at(c)
        spread = jnp.transpose(jnp.concatenate([log_in[c], jnp.zeros((120, both), F32)], axis=0))
        for u in todo:
            share = 1.0 / (1.0 + jnp.exp2(own_log[:, at[u]] - spread[:, u : u + 1]))
            mine_out = own[:, at[u]]
            win_b[:, at[u]] = (mine_out + (part_in[:, at[u]].astype(F32) - mine_out) * share).astype(BF16)
        r_win(c).start()
        l_win(c).start()
        return carry

    lax.fori_loop(0, CHUNKS, third, 0)

    def last(c, carry):
        r_lin(c).wait_recv()
        r_win(c).wait_recv()
        l_lin(c).wait()
        l_win(c).wait()
        return carry

    lax.fori_loop(0, CHUNKS, last, 0)

    x_lk().wait_send()
    x_lq().wait_send()
    for c in range(CHUNKS):
        x_v(c).wait_send()
        x_k(c).wait_send()
        x_q(c).wait_send()
        r_lin(c).wait_send()
        r_win(c).wait_send()

    @pl.when(has_prev)
    def _():
        for c in range(CHUNKS):
            z_q(c).wait_send()
            y_q(c).wait_send()

    @pl.when(has_next)
    def _():
        c_norm().wait_send()
        for c in range(CHUNKS):
            c_state(c).wait_send()
            p_out(c).wait_send()
            p_log(c).wait_send()


def on_device(linear_query, linear_key, values, window_query, window_key):
    rows, width = values.shape
    heads = linear_query.shape[1] // FEAT
    dim = width // heads
    pairs = lax.axis_size("seq") // 2
    half_heads = heads // 2
    half = width // 2
    lanes = half_heads * FEAT
    both = 2 * rows
    per = half_heads // CHUNKS
    state_type = BF16 if pairs <= 8 else F32
    dma = pltpu.SemaphoreType.DMA
    linear, window = pl.pallas_call(
        functools.partial(kernel, pairs, rows, dim, heads),
        out_shape=(
            jax.ShapeDtypeStruct((rows, width), BF16),
            jax.ShapeDtypeStruct((rows, width), BF16),
        ),
        in_specs=[pl.BlockSpec(memory_space=pl.ANY)] * 6,
        out_specs=(pl.BlockSpec(memory_space=pl.ANY),) * 2,
        scratch_shapes=[
            pltpu.VMEM((3, FEATS, lanes), BF16),
            pltpu.VMEM((rows, lanes), BF16),
            pltpu.VMEM((rows, lanes), BF16),
            pltpu.VMEM((rows, half), BF16),
            pltpu.VMEM((rows, half), BF16),
            pltpu.VMEM((rows, half), BF16),
            pltpu.VMEM((half_heads, both, FEATS), BF16),
            pltpu.VMEM((both, lanes), BF16),
            pltpu.VMEM((both, lanes), BF16),
            pltpu.VMEM((both, half), BF16),
            pltpu.VMEM((both, half), BF16),
            pltpu.VMEM((both, half), BF16),
            pltpu.VMEM((both, half), BF16),
            pltpu.VMEM((both, half), BF16),
            pltpu.VMEM((both, half), BF16),
            pltpu.VMEM((CHUNKS, 8, both), F32),
            pltpu.VMEM((CHUNKS, 8, both), F32),
            pltpu.VMEM((both, half), F32),
            pltpu.VMEM((both, half), F32),
            pltpu.VMEM((both, half), F32),
            pltpu.VMEM((both, half), F32),
            pltpu.VMEM((half_heads, FEATS, dim), F32),
            pltpu.VMEM((FEATS, 128), F32),
            pltpu.VMEM((CHUNKS, per, FEATS, dim), state_type),
            pltpu.VMEM((FEATS, 128), F32),
            pltpu.VMEM((CHUNKS, per, FEATS, dim), state_type),
            pltpu.VMEM((FEATS, 128), F32),
            pltpu.VMEM((both, half), BF16),
            pltpu.VMEM((both, half), BF16),
            pltpu.VMEM((2, both, both), F32),
            dma((2 + 3 * CHUNKS,)),
            dma((2 + 3 * CHUNKS,)),
            dma((2 * CHUNKS,)),
            dma((2 * CHUNKS,)),
            dma((2 * CHUNKS,)),
            dma((2 * CHUNKS,)),
            dma((CHUNKS + 1,)),
            dma((CHUNKS + 1,)),
            dma((2 * CHUNKS,)),
            dma((2 * CHUNKS,)),
            dma((11 + 2 * CHUNKS,)),
        ],
        compiler_params=pltpu.CompilerParams(
            collective_id=0, has_side_effects=True, vmem_limit_bytes=60 * 1024 * 1024
        ),
        cost_estimate=pl.CostEstimate(
            flops=4_000_000_000, bytes_accessed=4_000_000, transcendentals=1_600_000
        ),
    )(linear_query, linear_key, values, window_query, window_key, selections(lanes))
    return linear.astype(F32), window


def solution(mesh):
    spec = P(("grp", "seq"), None)
    return jax.shard_map(
        on_device,
        mesh=mesh,
        in_specs=(spec,) * 5,
        out_specs=(spec, spec),
        check_vma=False,
    )
```

```python
import functools
import jax
import jax.numpy as jnp
import numpy as np
from jax import lax
from jax.experimental import pallas as pl
from jax.experimental.pallas import tpu as pltpu
from jax.sharding import PartitionSpec as P

FEAT = 16
WINDOW = 256
PAIRS = FEAT * (FEAT + 1) // 2
FEATS = 160
ONE_ROW = PAIRS + FEAT
CHUNKS = 4
MESH = pl.DeviceIdType.MESH
F32 = jnp.float32
BF16 = jnp.bfloat16


def selections(lanes):
    lower, upper = np.triu_indices(FEAT)
    left = np.zeros((FEATS, FEAT), np.float32)
    right = np.zeros((FEATS, FEAT), np.float32)
    right_query = np.zeros((FEATS, FEAT), np.float32)
    rows = np.arange(PAIRS)
    left[rows, lower] = 1.0
    right[rows, upper] = 1.0
    right_query[rows, upper] = np.where(lower == upper, 1.0, 2.0)
    left[PAIRS + np.arange(FEAT), np.arange(FEAT)] = 1.0
    stacked = np.stack([left, right, right_query])
    return jnp.asarray(np.tile(stacked, (1, 1, lanes // FEAT)), BF16)


def dot_t(a, b):
    return lax.dot_general(a, b, (((1,), (1,)), ((), ())), preferred_element_type=F32)


def dot(a, b):
    return jnp.dot(a, b, preferred_element_type=F32)


def kernel(
    pairs, rows, dim, heads,
    lq_ref, lk_ref, v_ref, wq_ref, wk_ref, sel_in,
    lin_ref, win_ref,
    sel_ref, lqs, lks, vs, qs, ks, qf, lq2, lk2, v2, q2, k2, qn, part_out, part_in, log_out, log_in, own, own_log, num, den, state, norm, state_in, norm_in, state_out, norm_out,
    lin_b, win_b, bias,
    xs, xr, zs, zr, ps, pr, cs, cr, rs, rr, ls,
):
    me = lax.axis_index("seq")
    pair = me // 2
    par = me % 2
    other = 1 - par
    partner = {"seq": pair * 2 + other}
    ahead = {"seq": jnp.minimum(me + 2, 2 * pairs - 1)}
    behind = {"seq": jnp.maximum(me - 2, 0)}
    has_next = pair < pairs - 1
    has_prev = pair > 0
    half_heads = heads // 2
    half = half_heads * dim
    width = half // CHUNKS
    per = width // dim
    lanes = half_heads * FEAT
    mine = pl.ds(pl.multiple_of(par * rows, rows), rows)
    theirs = pl.ds(pl.multiple_of(other * rows, rows), rows)

    def own_cols(c):
        return pl.ds(pl.multiple_of(par * half + c * width, width), width)

    def cols(c):
        return pl.ds(c * width if isinstance(c, int) else pl.multiple_of(c * width, width), width)

    small_other = pl.ds(pl.multiple_of(other * lanes, lanes), lanes)
    small_own = pl.ds(pl.multiple_of(par * lanes, lanes), lanes)
    all_own = pl.ds(pl.multiple_of(par * half, half), half)
    all_other = pl.ds(pl.multiple_of(other * half, half), half)

    def local(src, dst, at):
        return pltpu.make_async_copy(src, dst, ls.at[at])

    fetched = [
        local(lk_ref.at[:, small_other], lks, 0),
        local(lq_ref.at[:, small_other], lqs, 1),
        local(v_ref.at[:, all_other], vs, 2),
        local(v_ref.at[:, all_own], v2.at[mine, :], 3),
        local(wk_ref.at[:, all_other], ks, 4),
        local(wk_ref.at[:, all_own], k2.at[mine, :], 5),
        local(wq_ref.at[:, all_other], qs, 6),
        local(wq_ref.at[:, all_own], q2.at[mine, :], 7),
        local(lk_ref.at[:, small_own], lk2.at[mine, :], 8),
        local(lq_ref.at[:, small_own], lq2.at[mine, :], 9),
        local(sel_in, sel_ref, 10),
    ]
    for copy in fetched:
        copy.start()

    barrier = pltpu.get_barrier_semaphore()
    pl.semaphore_signal(barrier, inc=1, device_id=partner, device_id_type=MESH)

    @pl.when(has_next)
    def _():
        pl.semaphore_signal(barrier, inc=1, device_id=ahead, device_id_type=MESH)

    @pl.when(has_prev)
    def _():
        pl.semaphore_signal(barrier, inc=1, device_id=behind, device_id_type=MESH)

    pl.semaphore_wait(barrier, 1 + jnp.minimum(pair, 1) + jnp.minimum(pairs - 1 - pair, 1))

    def remote(src, dst, send, recv, where):
        return pltpu.make_async_remote_copy(
            src_ref=src, dst_ref=dst, send_sem=send, recv_sem=recv,
            device_id=where, device_id_type=MESH,
        )

    def x_lk():
        return remote(lks, lk2.at[mine, :], xs.at[0], xr.at[0], partner)

    def x_lq():
        return remote(lqs, lq2.at[mine, :], xs.at[1], xr.at[1], partner)

    def x_copy(src, dst, slot, c):
        at = 2 + slot * CHUNKS + c
        return remote(src.at[:, cols(c)], dst.at[mine, cols(c)], xs.at[at], xr.at[at], partner)

    def x_v(c):
        return x_copy(vs, v2, 0, c)

    def x_k(c):
        return x_copy(ks, k2, 1, c)

    def x_q(c):
        return x_copy(qs, q2, 2, c)

    def z_q(c):
        return remote(q2.at[mine, cols(c)], qn.at[mine, cols(c)], zs.at[c], zr.at[c], behind)

    def y_q(c):
        at = CHUNKS + c
        return remote(q2.at[theirs, cols(c)], qn.at[theirs, cols(c)], zs.at[at], zr.at[at], behind)

    def p_out(c):
        return remote(part_out.at[:, cols(c)], part_in.at[:, cols(c)], ps.at[c], pr.at[c], ahead)

    def p_log(c):
        at = CHUNKS + c
        return remote(log_out.at[c], log_in.at[c], ps.at[at], pr.at[at], ahead)

    def c_state(c):
        return remote(state_out.at[c], state_in.at[c], cs.at[c], cr.at[c], ahead)

    def c_norm():
        return remote(norm_out, norm_in, cs.at[CHUNKS], cr.at[CHUNKS], ahead)

    def r_lin(c):
        return remote(lin_b.at[theirs, cols(c)], lin_ref.at[:, own_cols(c)], rs.at[c], rr.at[c], partner)

    def r_win(c):
        at = CHUNKS + c
        return remote(win_b.at[theirs, cols(c)], win_ref.at[:, own_cols(c)], rs.at[at], rr.at[at], partner)

    def l_lin(c):
        return local(lin_b.at[mine, cols(c)], lin_ref.at[:, own_cols(c)], 11 + c)

    def l_win(c):
        return local(win_b.at[mine, cols(c)], win_ref.at[:, own_cols(c)], 11 + CHUNKS + c)

    for copy in fetched:
        copy.wait()
    x_lk().start()
    x_lq().start()
    for c in range(CHUNKS):
        x_v(c).start()
    for c in range(CHUNKS):
        x_q(c).start()

        @pl.when(has_prev)
        def _():
            z_q(c).start()

    for c in range(CHUNKS):
        x_k(c).start()

    @pl.when(pair == 0)
    def _():
        part_in[...] = jnp.zeros_like(part_in)
        log_in[...] = jnp.full_like(log_in, -1e30)
        state_in[...] = jnp.zeros_like(state_in)
        norm_in[...] = jnp.zeros_like(norm_in)

    norm[...] = jnp.zeros_like(norm)
    both = 2 * rows
    row_at = lax.broadcasted_iota(jnp.int32, (both, both), 0)
    col_at = lax.broadcasted_iota(jnp.int32, (both, both), 1)
    causal = col_at <= row_at
    bias[0] = jnp.where(causal, 0.0, -1e30)
    bias[1] = jnp.where(causal, -1e30, 0.0)
    x_lk().wait_recv()
    x_lq().wait_recv()

    ones = jnp.ones((both, dim), BF16)
    lane = lax.broadcasted_iota(jnp.int32, (both, lanes), 1) // FEAT
    feat_row = lax.broadcasted_iota(jnp.int32, (FEATS, both), 0)
    row_left = jnp.where(feat_row == ONE_ROW, 1.0, 0.0)
    row_right = jnp.where((feat_row >= PAIRS) & (feat_row <= ONE_ROW), 1.0, 0.0)
    norm_lane = lax.broadcasted_iota(jnp.int32, (FEATS, 128), 1)

    feat_lane = lax.broadcasted_iota(jnp.int32, (both, FEATS), 1)
    lane_left = jnp.where(feat_lane == ONE_ROW, 1.0, 0.0)
    lane_right = jnp.where((feat_lane >= PAIRS) & (feat_lane <= ONE_ROW), 2.0, 0.0)

    def first(c, carry):
        x_v(c).wait_recv()
        todo = range(per)
        keys = lk2[...]
        head = [c * per + u for u in todo]
        at = [pl.ds(pl.multiple_of(head[u] * dim, dim), dim) for u in todo]
        key_m = [jnp.where(lane == head[u], keys.astype(F32), 0.0).astype(BF16) for u in todo]
        query_m = [jnp.where(lane == head[u], lq2[...].astype(F32) * 0.25, 0.0).astype(BF16) for u in todo]
        values = [jnp.concatenate([v2[:, at[u]], ones], axis=1) for u in todo]
        left = [dot_t(sel_ref[0], key_m[u]) for u in todo]
        right = [dot_t(sel_ref[1], key_m[u]) for u in todo]
        a = [dot_t(query_m[u], keys) + 1.0 for u in todo]
        feats = [((left[u] + row_left) * (right[u] + row_right)).astype(BF16) for u in todo]
        summed = [dot(feats[u], values[u]) for u in todo]
        weight = [jnp.where(causal, a[u] * a[u] + 1.0, 0.0).astype(BF16) for u in todo]
        mixed = [dot(weight[u], values[u]) for u in todo]
        for u in todo:
            state[head[u]] = summed[u][:, :dim]
            norm[...] += jnp.where(norm_lane == head[u], summed[u][:, dim:], 0.0)

        @pl.when(has_next & (pair == 0))
        def _():
            for u in todo:
                state_out[c, u] = summed[u][:, :dim].astype(state_out.dtype)
            c_state(c).start()

        left = [dot_t(query_m[u], sel_ref[0]) for u in todo]
        right = [dot_t(query_m[u], sel_ref[2]) for u in todo]
        for u in todo:
            num[:, at[u]] = mixed[u][:, :dim]
            den[:, at[u]] = mixed[u][:, dim:]
            qf[head[u]] = ((left[u] + lane_left) * (right[u] + lane_right)).astype(BF16)
        return carry

    lax.fori_loop(0, CHUNKS, first, 0)

    def chain(c):
        @pl.when(has_prev)
        def _():
            c_state(c).wait_recv()

        @pl.when(has_prev & has_next)
        def _():
            total = state_in[c].astype(F32) + state[pl.ds(c * per, per)]
            state_out[c] = total.astype(state_out.dtype)
            c_state(c).start()

    early = CHUNKS // 2
    for c in range(CHUNKS):
        x_q(c).wait_recv()

        @pl.when(has_prev)
        def _():
            y_q(c).start()

        if c < early:
            chain(c)

    @pl.when(has_prev)
    def _():
        c_norm().wait_recv()

    @pl.when(has_next)
    def _():
        norm_out[...] = norm_in[...] + norm[...]
        c_norm().start()

    factor = dim ** -0.5 * 1.4426950408889634
    head_lane = lax.broadcasted_iota(jnp.int32, (both, 128), 1)
    todo = range(per)

    def heads_at(c):
        head = [c * per + u for u in todo]
        return head, [pl.ds(pl.multiple_of(head[u] * dim, dim), dim) for u in todo]

    def attend(queries, at, which):
        scores = [dot_t(queries[:, at[u]], k2[:, at[u]]) for u in todo]
        scores = [scores[u] * factor + bias[which] for u in todo]
        largest = [jnp.max(scores[u], axis=1, keepdims=True) for u in todo]
        weights = [jnp.exp2(scores[u] - largest[u]).astype(BF16) for u in todo]
        mixed = [dot(weights[u], jnp.concatenate([v2[:, at[u]], ones], axis=1)) for u in todo]
        outs = [mixed[u][:, :dim] / mixed[u][:, dim:] for u in todo]
        return outs, [largest[u] + jnp.log2(mixed[u][:, dim:]) for u in todo]

    def merge(c):
        @pl.when(has_prev)
        def _():
            p_out(c).wait_recv()
            p_log(c).wait_recv()

        head, at = heads_at(c)
        spread = jnp.transpose(jnp.concatenate([log_in[c], jnp.zeros((120, both), F32)], axis=0))
        for u in todo:
            share = 1.0 / (1.0 + jnp.exp2(own_log[:, at[u]] - spread[:, u : u + 1]))
            mine_out = own[:, at[u]]
            win_b[:, at[u]] = (mine_out + (part_in[:, at[u]].astype(F32) - mine_out) * share).astype(BF16)
        r_win(c).start()
        l_win(c).start()

    def second(c, carry):
        x_k(c).wait_recv()

        @pl.when(c < CHUNKS - early)
        def _():
            chain(c + early)

        head, at = heads_at(c)
        outs, logs = attend(q2, at, 0)
        added = []
        for u in todo:
            norm_col = jnp.sum(jnp.where(norm_lane == head[u], norm_in[...], 0.0), axis=1, keepdims=True)
            prior = jnp.concatenate(
                [state_in[c, u].astype(BF16), jnp.broadcast_to(norm_col, (FEATS, dim)).astype(BF16)], axis=1
            )
            added.append(dot(qf[head[u]], prior))
        for u in todo:
            own[:, at[u]] = outs[u]
            own_log[:, at[u]] = logs[u]
            linear = (num[:, at[u]] + added[u][:, :dim]) / (den[:, at[u]] + added[u][:, dim:])
            lin_b[:, at[u]] = linear.astype(BF16)
        r_lin(c).start()
        l_lin(c).start()

        @pl.when(has_next)
        def _():
            z_q(c).wait_recv()
            y_q(c).wait_recv()
            outs, logs = attend(qn, at, 1)
            packed = jnp.zeros((both, 128), F32)
            for u in todo:
                part_out[:, at[u]] = outs[u].astype(BF16)
                packed = jnp.where(head_lane == u, logs[u], packed)
            log_out[c] = jnp.transpose(packed)[:8]
            p_out(c).start()
            p_log(c).start()

        @pl.when(c > 0)
        def _():
            merge(c - 1)

        return carry

    lax.fori_loop(0, CHUNKS, second, 0)

    merge(CHUNKS - 1)

    def last(c, carry):
        r_lin(c).wait_recv()
        r_win(c).wait_recv()
        l_lin(c).wait()
        l_win(c).wait()
        return carry

    lax.fori_loop(0, CHUNKS, last, 0)

    x_lk().wait_send()
    x_lq().wait_send()
    for c in range(CHUNKS):
        x_v(c).wait_send()
        x_k(c).wait_send()
        x_q(c).wait_send()
        r_lin(c).wait_send()
        r_win(c).wait_send()

    @pl.when(has_prev)
    def _():
        for c in range(CHUNKS):
            z_q(c).wait_send()
            y_q(c).wait_send()

    @pl.when(has_next)
    def _():
        c_norm().wait_send()
        for c in range(CHUNKS):
            c_state(c).wait_send()
            p_out(c).wait_send()
            p_log(c).wait_send()


def on_device(linear_query, linear_key, values, window_query, window_key):
    rows, width = values.shape
    heads = linear_query.shape[1] // FEAT
    dim = width // heads
    pairs = lax.axis_size("seq") // 2
    half_heads = heads // 2
    half = width // 2
    lanes = half_heads * FEAT
    both = 2 * rows
    per = half_heads // CHUNKS
    state_type = BF16 if pairs <= 8 else F32
    dma = pltpu.SemaphoreType.DMA
    linear, window = pl.pallas_call(
        functools.partial(kernel, pairs, rows, dim, heads),
        out_shape=(
            jax.ShapeDtypeStruct((rows, width), BF16),
            jax.ShapeDtypeStruct((rows, width), BF16),
        ),
        in_specs=[pl.BlockSpec(memory_space=pl.ANY)] * 6,
        out_specs=(pl.BlockSpec(memory_space=pl.ANY),) * 2,
        scratch_shapes=[
            pltpu.VMEM((3, FEATS, lanes), BF16),
            pltpu.VMEM((rows, lanes), BF16),
            pltpu.VMEM((rows, lanes), BF16),
            pltpu.VMEM((rows, half), BF16),
            pltpu.VMEM((rows, half), BF16),
            pltpu.VMEM((rows, half), BF16),
            pltpu.VMEM((half_heads, both, FEATS), BF16),
            pltpu.VMEM((both, lanes), BF16),
            pltpu.VMEM((both, lanes), BF16),
            pltpu.VMEM((both, half), BF16),
            pltpu.VMEM((both, half), BF16),
            pltpu.VMEM((both, half), BF16),
            pltpu.VMEM((both, half), BF16),
            pltpu.VMEM((both, half), BF16),
            pltpu.VMEM((both, half), BF16),
            pltpu.VMEM((CHUNKS, 8, both), F32),
            pltpu.VMEM((CHUNKS, 8, both), F32),
            pltpu.VMEM((both, half), F32),
            pltpu.VMEM((both, half), F32),
            pltpu.VMEM((both, half), F32),
            pltpu.VMEM((both, half), F32),
            pltpu.VMEM((half_heads, FEATS, dim), F32),
            pltpu.VMEM((FEATS, 128), F32),
            pltpu.VMEM((CHUNKS, per, FEATS, dim), state_type),
            pltpu.VMEM((FEATS, 128), F32),
            pltpu.VMEM((CHUNKS, per, FEATS, dim), state_type),
            pltpu.VMEM((FEATS, 128), F32),
            pltpu.VMEM((both, half), BF16),
            pltpu.VMEM((both, half), BF16),
            pltpu.VMEM((2, both, both), F32),
            dma((2 + 3 * CHUNKS,)),
            dma((2 + 3 * CHUNKS,)),
            dma((2 * CHUNKS,)),
            dma((2 * CHUNKS,)),
            dma((2 * CHUNKS,)),
            dma((2 * CHUNKS,)),
            dma((CHUNKS + 1,)),
            dma((CHUNKS + 1,)),
            dma((2 * CHUNKS,)),
            dma((2 * CHUNKS,)),
            dma((11 + 2 * CHUNKS,)),
        ],
        compiler_params=pltpu.CompilerParams(
            collective_id=0, has_side_effects=True, vmem_limit_bytes=60 * 1024 * 1024
        ),
        cost_estimate=pl.CostEstimate(
            flops=4_000_000_000, bytes_accessed=4_000_000, transcendentals=1_600_000
        ),
    )(linear_query, linear_key, values, window_query, window_key, selections(lanes))
    return linear.astype(F32), window


def solution(mesh):
    spec = P(("grp", "seq"), None)
    return jax.shard_map(
        on_device,
        mesh=mesh,
        in_specs=(spec,) * 5,
        out_specs=(spec, spec),
        check_vma=False,
    )
```

```python
import functools
import jax
import jax.numpy as jnp
import numpy as np
from jax import lax
from jax.experimental import pallas as pl
from jax.experimental.pallas import tpu as pltpu
from jax.sharding import PartitionSpec as P

FEAT = 16
WINDOW = 256
PAIRS = FEAT * (FEAT + 1) // 2
FEATS = 160
ONE_ROW = PAIRS + FEAT
CHUNKS = 4
MESH = pl.DeviceIdType.MESH
F32 = jnp.float32
BF16 = jnp.bfloat16


def selections(lanes):
    lower, upper = np.triu_indices(FEAT)
    left = np.zeros((FEATS, FEAT), np.float32)
    right = np.zeros((FEATS, FEAT), np.float32)
    right_query = np.zeros((FEATS, FEAT), np.float32)
    rows = np.arange(PAIRS)
    left[rows, lower] = 1.0
    right[rows, upper] = 1.0
    right_query[rows, upper] = np.where(lower == upper, 1.0, 2.0)
    left[PAIRS + np.arange(FEAT), np.arange(FEAT)] = 1.0
    stacked = np.stack([left, right, right_query])
    return jnp.asarray(np.tile(stacked, (1, 1, lanes // FEAT)), BF16)


def dot_t(a, b):
    return lax.dot_general(a, b, (((1,), (1,)), ((), ())), preferred_element_type=F32)


def dot(a, b):
    return jnp.dot(a, b, preferred_element_type=F32)


def kernel(
    pairs, rows, dim, heads,
    lq_ref, lk_ref, v_ref, wq_ref, wk_ref, sel_in,
    lin_ref, win_ref,
    sel_ref, lqs, lks, vs, qs, ks, qf, lq2, lk2, v2, q2, k2, qn, part_out, part_in, log_out, log_in, own, own_log, num, den, state, norm, state_in, norm_in, state_out, norm_out,
    lin_b, win_b, bias,
    xs, xr, zs, zr, ps, pr, cs, cr, rs, rr, ls,
):
    me = lax.axis_index("seq")
    pair = me // 2
    par = me % 2
    other = 1 - par
    partner = {"seq": pair * 2 + other}
    ahead = {"seq": jnp.minimum(me + 2, 2 * pairs - 1)}
    behind = {"seq": jnp.maximum(me - 2, 0)}
    has_next = pair < pairs - 1
    has_prev = pair > 0
    half_heads = heads // 2
    half = half_heads * dim
    width = half // CHUNKS
    per = width // dim
    lanes = half_heads * FEAT
    mine = pl.ds(pl.multiple_of(par * rows, rows), rows)
    theirs = pl.ds(pl.multiple_of(other * rows, rows), rows)

    def own_cols(c):
        return pl.ds(pl.multiple_of(par * half + c * width, width), width)

    def cols(c):
        return pl.ds(c * width if isinstance(c, int) else pl.multiple_of(c * width, width), width)

    small_other = pl.ds(pl.multiple_of(other * lanes, lanes), lanes)
    small_own = pl.ds(pl.multiple_of(par * lanes, lanes), lanes)
    all_own = pl.ds(pl.multiple_of(par * half, half), half)
    all_other = pl.ds(pl.multiple_of(other * half, half), half)

    def local(src, dst, at):
        return pltpu.make_async_copy(src, dst, ls.at[at])

    fetched = [
        local(lk_ref.at[:, small_other], lks, 0),
        local(lq_ref.at[:, small_other], lqs, 1),
        local(v_ref.at[:, all_other], vs, 2),
        local(v_ref.at[:, all_own], v2.at[mine, :], 3),
        local(wk_ref.at[:, all_other], ks, 4),
        local(wk_ref.at[:, all_own], k2.at[mine, :], 5),
        local(wq_ref.at[:, all_other], qs, 6),
        local(wq_ref.at[:, all_own], q2.at[mine, :], 7),
        local(lk_ref.at[:, small_own], lk2.at[mine, :], 8),
        local(lq_ref.at[:, small_own], lq2.at[mine, :], 9),
        local(sel_in, sel_ref, 10),
    ]
    for copy in fetched:
        copy.start()

    barrier = pltpu.get_barrier_semaphore()
    pl.semaphore_signal(barrier, inc=1, device_id=partner, device_id_type=MESH)

    @pl.when(has_next)
    def _():
        pl.semaphore_signal(barrier, inc=1, device_id=ahead, device_id_type=MESH)

    @pl.when(has_prev)
    def _():
        pl.semaphore_signal(barrier, inc=1, device_id=behind, device_id_type=MESH)

    pl.semaphore_wait(barrier, 1 + jnp.minimum(pair, 1) + jnp.minimum(pairs - 1 - pair, 1))

    def remote(src, dst, send, recv, where):
        return pltpu.make_async_remote_copy(
            src_ref=src, dst_ref=dst, send_sem=send, recv_sem=recv,
            device_id=where, device_id_type=MESH,
        )

    def x_lk():
        return remote(lks, lk2.at[mine, :], xs.at[0], xr.at[0], partner)

    def x_lq():
        return remote(lqs, lq2.at[mine, :], xs.at[1], xr.at[1], partner)

    def x_copy(src, dst, slot, c):
        at = 2 + slot * CHUNKS + c
        return remote(src.at[:, cols(c)], dst.at[mine, cols(c)], xs.at[at], xr.at[at], partner)

    def x_v(c):
        return x_copy(vs, v2, 0, c)

    def x_k(c):
        return x_copy(ks, k2, 1, c)

    def x_q(c):
        return x_copy(qs, q2, 2, c)

    def z_q(c):
        return remote(q2.at[mine, cols(c)], qn.at[mine, cols(c)], zs.at[c], zr.at[c], behind)

    def y_q(c):
        at = CHUNKS + c
        return remote(q2.at[theirs, cols(c)], qn.at[theirs, cols(c)], zs.at[at], zr.at[at], behind)

    def p_out(c):
        return remote(part_out.at[:, cols(c)], part_in.at[:, cols(c)], ps.at[c], pr.at[c], ahead)

    def p_log(c):
        at = CHUNKS + c
        return remote(log_out.at[c], log_in.at[c], ps.at[at], pr.at[at], ahead)

    def c_state(c):
        return remote(state_out.at[c], state_in.at[c], cs.at[c], cr.at[c], ahead)

    def c_norm():
        return remote(norm_out, norm_in, cs.at[CHUNKS], cr.at[CHUNKS], ahead)

    def r_lin(c):
        return remote(lin_b.at[theirs, cols(c)], lin_ref.at[:, own_cols(c)], rs.at[c], rr.at[c], partner)

    def r_win(c):
        at = CHUNKS + c
        return remote(win_b.at[theirs, cols(c)], win_ref.at[:, own_cols(c)], rs.at[at], rr.at[at], partner)

    def l_lin(c):
        return local(lin_b.at[mine, cols(c)], lin_ref.at[:, own_cols(c)], 11 + c)

    def l_win(c):
        return local(win_b.at[mine, cols(c)], win_ref.at[:, own_cols(c)], 11 + CHUNKS + c)

    for copy in fetched:
        copy.wait()
    x_lk().start()
    x_lq().start()
    for c in range(CHUNKS):
        x_v(c).start()
    for c in range(CHUNKS):
        x_q(c).start()

        @pl.when(has_prev)
        def _():
            z_q(c).start()

    for c in range(CHUNKS):
        x_k(c).start()

    @pl.when(pair == 0)
    def _():
        part_in[...] = jnp.zeros_like(part_in)
        log_in[...] = jnp.full_like(log_in, -1e30)
        state_in[...] = jnp.zeros_like(state_in)
        norm_in[...] = jnp.zeros_like(norm_in)

    norm[...] = jnp.zeros_like(norm)
    both = 2 * rows
    row_at = lax.broadcasted_iota(jnp.int32, (both, both), 0)
    col_at = lax.broadcasted_iota(jnp.int32, (both, both), 1)
    causal = col_at <= row_at
    bias[0] = jnp.where(causal, 0.0, -1e30)
    bias[1] = jnp.where(causal, -1e30, 0.0)
    x_lk().wait_recv()
    x_lq().wait_recv()

    ones = jnp.ones((both, dim), BF16)
    lane = lax.broadcasted_iota(jnp.int32, (both, lanes), 1) // FEAT
    feat_row = lax.broadcasted_iota(jnp.int32, (FEATS, both), 0)
    row_left = jnp.where(feat_row == ONE_ROW, 1.0, 0.0)
    row_right = jnp.where((feat_row >= PAIRS) & (feat_row <= ONE_ROW), 1.0, 0.0)
    norm_lane = lax.broadcasted_iota(jnp.int32, (FEATS, 128), 1)

    feat_lane = lax.broadcasted_iota(jnp.int32, (both, FEATS), 1)
    lane_left = jnp.where(feat_lane == ONE_ROW, 1.0, 0.0)
    lane_right = jnp.where((feat_lane >= PAIRS) & (feat_lane <= ONE_ROW), 2.0, 0.0)

    def first(c, carry):
        x_v(c).wait_recv()
        todo = range(per)
        keys = lk2[...]
        head = [c * per + u for u in todo]
        at = [pl.ds(pl.multiple_of(head[u] * dim, dim), dim) for u in todo]
        key_m = [jnp.where(lane == head[u], keys.astype(F32), 0.0).astype(BF16) for u in todo]
        query_m = [jnp.where(lane == head[u], lq2[...].astype(F32) * 0.25, 0.0).astype(BF16) for u in todo]
        values = [jnp.concatenate([v2[:, at[u]], ones], axis=1) for u in todo]
        left = [dot_t(sel_ref[0], key_m[u]) for u in todo]
        right = [dot_t(sel_ref[1], key_m[u]) for u in todo]
        a = [dot_t(query_m[u], keys) + 1.0 for u in todo]
        feats = [((left[u] + row_left) * (right[u] + row_right)).astype(BF16) for u in todo]
        summed = [dot(feats[u], values[u]) for u in todo]
        weight = [jnp.where(causal, a[u] * a[u] + 1.0, 0.0).astype(BF16) for u in todo]
        mixed = [dot(weight[u], values[u]) for u in todo]
        for u in todo:
            state[head[u]] = summed[u][:, :dim]
            norm[...] += jnp.where(norm_lane == head[u], summed[u][:, dim:], 0.0)

        @pl.when(has_next & (pair == 0))
        def _():
            for u in todo:
                state_out[c, u] = summed[u][:, :dim].astype(state_out.dtype)
            c_state(c).start()

        left = [dot_t(query_m[u], sel_ref[0]) for u in todo]
        right = [dot_t(query_m[u], sel_ref[2]) for u in todo]
        for u in todo:
            num[:, at[u]] = mixed[u][:, :dim]
            den[:, at[u]] = mixed[u][:, dim:]
            qf[head[u]] = ((left[u] + lane_left) * (right[u] + lane_right)).astype(BF16)
        return carry

    lax.fori_loop(0, CHUNKS, first, 0)

    def chain(c):
        c_state(c).wait_recv()
        total = state_in[c].astype(F32) + state[pl.ds(c * per, per)]
        state_out[c] = total.astype(state_out.dtype)
        c_state(c).start()

    def chain_norm():
        c_norm().wait_recv()
        norm_out[...] = norm_in[...] + norm[...]
        c_norm().start()

    @pl.when(has_next & (pair == 0))
    def _():
        norm_out[...] = norm[...]
        c_norm().start()

    early = CHUNKS // 2
    for c in range(CHUNKS):
        x_q(c).wait_recv()

        @pl.when(has_prev)
        def _():
            y_q(c).start()

        @pl.when(has_next & (pair == 1))
        def _():
            chain(c)
            if c == 1:
                chain_norm()

    @pl.when(has_next & (pair >= 2))
    def _():
        for c in range(early):
            chain(c)
        chain_norm()

    factor = dim ** -0.5 * 1.4426950408889634
    head_lane = lax.broadcasted_iota(jnp.int32, (both, 128), 1)
    todo = range(per)

    def heads_at(c):
        head = [c * per + u for u in todo]
        return head, [pl.ds(pl.multiple_of(head[u] * dim, dim), dim) for u in todo]

    def attend(queries, at, which):
        scores = [dot_t(queries[:, at[u]], k2[:, at[u]]) for u in todo]
        scores = [scores[u] * factor + bias[which] for u in todo]
        largest = [jnp.max(scores[u], axis=1, keepdims=True) for u in todo]
        weights = [jnp.exp2(scores[u] - largest[u]).astype(BF16) for u in todo]
        mixed = [dot(weights[u], jnp.concatenate([v2[:, at[u]], ones], axis=1)) for u in todo]
        outs = [mixed[u][:, :dim] / mixed[u][:, dim:] for u in todo]
        return outs, [largest[u] + jnp.log2(mixed[u][:, dim:]) for u in todo]

    def merge(c):
        @pl.when(has_prev)
        def _():
            p_out(c).wait_recv()
            p_log(c).wait_recv()

        head, at = heads_at(c)
        spread = jnp.transpose(jnp.concatenate([log_in[c], jnp.zeros((120, both), F32)], axis=0))
        for u in todo:
            share = 1.0 / (1.0 + jnp.exp2(own_log[:, at[u]] - spread[:, u : u + 1]))
            mine_out = own[:, at[u]]
            win_b[:, at[u]] = (mine_out + (part_in[:, at[u]].astype(F32) - mine_out) * share).astype(BF16)
        r_win(c).start()
        l_win(c).start()

    def second(c, carry):
        x_k(c).wait_recv()

        head, at = heads_at(c)
        outs, logs = attend(q2, at, 0)

        last_pair = has_prev & (pair == pairs - 1)

        @pl.when(last_pair)
        def _():
            c_state(c).wait_recv()

        @pl.when(last_pair & (c == 0))
        def _():
            c_norm().wait_recv()

        added = []
        for u in todo:
            norm_col = jnp.sum(jnp.where(norm_lane == head[u], norm_in[...], 0.0), axis=1, keepdims=True)
            prior = jnp.concatenate(
                [state_in[c, u].astype(BF16), jnp.broadcast_to(norm_col, (FEATS, dim)).astype(BF16)], axis=1
            )
            added.append(dot(qf[head[u]], prior))
        for u in todo:
            own[:, at[u]] = outs[u]
            own_log[:, at[u]] = logs[u]
            linear = (num[:, at[u]] + added[u][:, :dim]) / (den[:, at[u]] + added[u][:, dim:])
            lin_b[:, at[u]] = linear.astype(BF16)
        r_lin(c).start()
        l_lin(c).start()

        @pl.when(has_next)
        def _():
            z_q(c).wait_recv()
            y_q(c).wait_recv()
            outs, logs = attend(qn, at, 1)
            packed = jnp.zeros((both, 128), F32)
            for u in todo:
                part_out[:, at[u]] = outs[u].astype(BF16)
                packed = jnp.where(head_lane == u, logs[u], packed)
            log_out[c] = jnp.transpose(packed)[:8]
            p_out(c).start()
            p_log(c).start()

        @pl.when(has_next & (pair >= 2) & (c == 0))
        def _():
            for late in range(early, CHUNKS):
                chain(late)

        @pl.when(c > 0)
        def _():
            merge(c - 1)

        return carry

    lax.fori_loop(0, CHUNKS, second, 0)

    merge(CHUNKS - 1)

    def last(c, carry):
        r_lin(c).wait_recv()
        r_win(c).wait_recv()
        l_lin(c).wait()
        l_win(c).wait()
        return carry

    lax.fori_loop(0, CHUNKS, last, 0)

    x_lk().wait_send()
    x_lq().wait_send()
    for c in range(CHUNKS):
        x_v(c).wait_send()
        x_k(c).wait_send()
        x_q(c).wait_send()
        r_lin(c).wait_send()
        r_win(c).wait_send()

    @pl.when(has_prev)
    def _():
        for c in range(CHUNKS):
            z_q(c).wait_send()
            y_q(c).wait_send()

    @pl.when(has_next)
    def _():
        c_norm().wait_send()
        for c in range(CHUNKS):
            c_state(c).wait_send()
            p_out(c).wait_send()
            p_log(c).wait_send()


def on_device(linear_query, linear_key, values, window_query, window_key):
    rows, width = values.shape
    heads = linear_query.shape[1] // FEAT
    dim = width // heads
    pairs = lax.axis_size("seq") // 2
    half_heads = heads // 2
    half = width // 2
    lanes = half_heads * FEAT
    both = 2 * rows
    per = half_heads // CHUNKS
    state_type = BF16 if pairs <= 8 else F32
    dma = pltpu.SemaphoreType.DMA
    linear, window = pl.pallas_call(
        functools.partial(kernel, pairs, rows, dim, heads),
        out_shape=(
            jax.ShapeDtypeStruct((rows, width), BF16),
            jax.ShapeDtypeStruct((rows, width), BF16),
        ),
        in_specs=[pl.BlockSpec(memory_space=pl.ANY)] * 6,
        out_specs=(pl.BlockSpec(memory_space=pl.ANY),) * 2,
        scratch_shapes=[
            pltpu.VMEM((3, FEATS, lanes), BF16),
            pltpu.VMEM((rows, lanes), BF16),
            pltpu.VMEM((rows, lanes), BF16),
            pltpu.VMEM((rows, half), BF16),
            pltpu.VMEM((rows, half), BF16),
            pltpu.VMEM((rows, half), BF16),
            pltpu.VMEM((half_heads, both, FEATS), BF16),
            pltpu.VMEM((both, lanes), BF16),
            pltpu.VMEM((both, lanes), BF16),
            pltpu.VMEM((both, half), BF16),
            pltpu.VMEM((both, half), BF16),
            pltpu.VMEM((both, half), BF16),
            pltpu.VMEM((both, half), BF16),
            pltpu.VMEM((both, half), BF16),
            pltpu.VMEM((both, half), BF16),
            pltpu.VMEM((CHUNKS, 8, both), F32),
            pltpu.VMEM((CHUNKS, 8, both), F32),
            pltpu.VMEM((both, half), F32),
            pltpu.VMEM((both, half), F32),
            pltpu.VMEM((both, half), F32),
            pltpu.VMEM((both, half), F32),
            pltpu.VMEM((half_heads, FEATS, dim), F32),
            pltpu.VMEM((FEATS, 128), F32),
            pltpu.VMEM((CHUNKS, per, FEATS, dim), state_type),
            pltpu.VMEM((FEATS, 128), F32),
            pltpu.VMEM((CHUNKS, per, FEATS, dim), state_type),
            pltpu.VMEM((FEATS, 128), F32),
            pltpu.VMEM((both, half), BF16),
            pltpu.VMEM((both, half), BF16),
            pltpu.VMEM((2, both, both), F32),
            dma((2 + 3 * CHUNKS,)),
            dma((2 + 3 * CHUNKS,)),
            dma((2 * CHUNKS,)),
            dma((2 * CHUNKS,)),
            dma((2 * CHUNKS,)),
            dma((2 * CHUNKS,)),
            dma((CHUNKS + 1,)),
            dma((CHUNKS + 1,)),
            dma((2 * CHUNKS,)),
            dma((2 * CHUNKS,)),
            dma((11 + 2 * CHUNKS,)),
        ],
        compiler_params=pltpu.CompilerParams(
            collective_id=0, has_side_effects=True, vmem_limit_bytes=60 * 1024 * 1024
        ),
        cost_estimate=pl.CostEstimate(
            flops=4_000_000_000, bytes_accessed=4_000_000, transcendentals=1_600_000
        ),
    )(linear_query, linear_key, values, window_query, window_key, selections(lanes))
    return linear.astype(F32), window


def solution(mesh):
    spec = P(("grp", "seq"), None)
    return jax.shard_map(
        on_device,
        mesh=mesh,
        in_specs=(spec,) * 5,
        out_specs=(spec, spec),
        check_vma=False,
    )
```

```python
import functools
import jax
import jax.numpy as jnp
import numpy as np
from jax import lax
from jax.experimental import pallas as pl
from jax.experimental.pallas import tpu as pltpu
from jax.sharding import PartitionSpec as P

FEAT = 16
WINDOW = 256
PAIRS = FEAT * (FEAT + 1) // 2
FEATS = 160
ONE_ROW = PAIRS + FEAT
CHUNKS = 4
MESH = pl.DeviceIdType.MESH
F32 = jnp.float32
BF16 = jnp.bfloat16


def selections(lanes):
    lower, upper = np.triu_indices(FEAT)
    left = np.zeros((FEATS, FEAT), np.float32)
    right = np.zeros((FEATS, FEAT), np.float32)
    right_query = np.zeros((FEATS, FEAT), np.float32)
    rows = np.arange(PAIRS)
    left[rows, lower] = 1.0
    right[rows, upper] = 1.0
    right_query[rows, upper] = np.where(lower == upper, 1.0, 2.0)
    left[PAIRS + np.arange(FEAT), np.arange(FEAT)] = 1.0
    stacked = np.stack([left, right, right_query])
    return jnp.asarray(np.tile(stacked, (1, 1, lanes // FEAT)), BF16)


def dot_t(a, b):
    return lax.dot_general(a, b, (((1,), (1,)), ((), ())), preferred_element_type=F32)


def dot(a, b):
    return jnp.dot(a, b, preferred_element_type=F32)


def kernel(
    pairs, rows, dim, heads,
    lq_ref, lk_ref, v_ref, wq_ref, wk_ref, sel_in,
    lin_ref, win_ref,
    sel_ref, lqs, lks, vs, qs, ks, qf, lq2, lk2, v2, q2, k2, qn, part_out, part_in, log_out, log_in, own, own_log, num, den, state, norm, state_in, norm_in, state_out, norm_out,
    lin_b, win_b, bias,
    xs, xr, zs, zr, ps, pr, cs, cr, rs, rr, ls,
):
    me = lax.axis_index("seq")
    pair = me // 2
    par = me % 2
    other = 1 - par
    partner = {"seq": pair * 2 + other}
    ahead = {"seq": jnp.minimum(me + 2, 2 * pairs - 1)}
    behind = {"seq": jnp.maximum(me - 2, 0)}
    has_next = pair < pairs - 1
    has_prev = pair > 0
    half_heads = heads // 2
    half = half_heads * dim
    width = half // CHUNKS
    per = width // dim
    lanes = half_heads * FEAT
    mine = pl.ds(pl.multiple_of(par * rows, rows), rows)
    theirs = pl.ds(pl.multiple_of(other * rows, rows), rows)

    def own_cols(c):
        return pl.ds(pl.multiple_of(par * half + c * width, width), width)

    def cols(c):
        return pl.ds(c * width if isinstance(c, int) else pl.multiple_of(c * width, width), width)

    small_other = pl.ds(pl.multiple_of(other * lanes, lanes), lanes)
    small_own = pl.ds(pl.multiple_of(par * lanes, lanes), lanes)
    all_own = pl.ds(pl.multiple_of(par * half, half), half)
    all_other = pl.ds(pl.multiple_of(other * half, half), half)

    def local(src, dst, at):
        return pltpu.make_async_copy(src, dst, ls.at[at])

    fetched = [
        local(lk_ref.at[:, small_other], lks, 0),
        local(lq_ref.at[:, small_other], lqs, 1),
        local(v_ref.at[:, all_other], vs, 2),
        local(v_ref.at[:, all_own], v2.at[mine, :], 3),
        local(wk_ref.at[:, all_other], ks, 4),
        local(wk_ref.at[:, all_own], k2.at[mine, :], 5),
        local(wq_ref.at[:, all_other], qs, 6),
        local(wq_ref.at[:, all_own], q2.at[mine, :], 7),
        local(lk_ref.at[:, small_own], lk2.at[mine, :], 8),
        local(lq_ref.at[:, small_own], lq2.at[mine, :], 9),
        local(sel_in, sel_ref, 10),
    ]
    for copy in fetched:
        copy.start()

    barrier = pltpu.get_barrier_semaphore()
    pl.semaphore_signal(barrier, inc=1, device_id=partner, device_id_type=MESH)

    @pl.when(has_next)
    def _():
        pl.semaphore_signal(barrier, inc=1, device_id=ahead, device_id_type=MESH)

    @pl.when(has_prev)
    def _():
        pl.semaphore_signal(barrier, inc=1, device_id=behind, device_id_type=MESH)

    pl.semaphore_wait(barrier, 1 + jnp.minimum(pair, 1) + jnp.minimum(pairs - 1 - pair, 1))

    def remote(src, dst, send, recv, where):
        return pltpu.make_async_remote_copy(
            src_ref=src, dst_ref=dst, send_sem=send, recv_sem=recv,
            device_id=where, device_id_type=MESH,
        )

    def x_lk():
        return remote(lks, lk2.at[mine, :], xs.at[0], xr.at[0], partner)

    def x_lq():
        return remote(lqs, lq2.at[mine, :], xs.at[1], xr.at[1], partner)

    def x_copy(src, dst, slot, c):
        at = 2 + slot * CHUNKS + c
        return remote(src.at[:, cols(c)], dst.at[mine, cols(c)], xs.at[at], xr.at[at], partner)

    def x_v(c):
        return x_copy(vs, v2, 0, c)

    def x_k(c):
        return x_copy(ks, k2, 1, c)

    def x_q(c):
        return x_copy(qs, q2, 2, c)

    def z_q(c):
        return remote(q2.at[mine, cols(c)], qn.at[mine, cols(c)], zs.at[c], zr.at[c], behind)

    def y_q(c):
        at = CHUNKS + c
        return remote(q2.at[theirs, cols(c)], qn.at[theirs, cols(c)], zs.at[at], zr.at[at], behind)

    def p_out(c):
        return remote(part_out.at[:, cols(c)], part_in.at[:, cols(c)], ps.at[c], pr.at[c], ahead)

    def p_log(c):
        at = CHUNKS + c
        return remote(log_out.at[c], log_in.at[c], ps.at[at], pr.at[at], ahead)

    def c_state(c):
        return remote(state_out.at[c], state_in.at[c], cs.at[c], cr.at[c], ahead)

    def c_norm():
        return remote(norm_out, norm_in, cs.at[CHUNKS], cr.at[CHUNKS], ahead)

    def r_lin(c):
        return remote(lin_b.at[theirs, cols(c)], lin_ref.at[:, own_cols(c)], rs.at[c], rr.at[c], partner)

    def r_win(c):
        at = CHUNKS + c
        return remote(win_b.at[theirs, cols(c)], win_ref.at[:, own_cols(c)], rs.at[at], rr.at[at], partner)

    def l_lin(c):
        return local(lin_b.at[mine, cols(c)], lin_ref.at[:, own_cols(c)], 11 + c)

    def l_win(c):
        return local(win_b.at[mine, cols(c)], win_ref.at[:, own_cols(c)], 11 + CHUNKS + c)

    for copy in fetched:
        copy.wait()
    x_lk().start()
    x_lq().start()
    for c in range(CHUNKS):
        x_v(c).start()
    for c in range(CHUNKS):
        x_q(c).start()

        @pl.when(has_prev)
        def _():
            z_q(c).start()

    for c in range(CHUNKS):
        x_k(c).start()

    @pl.when(pair == 0)
    def _():
        part_in[...] = jnp.zeros_like(part_in)
        log_in[...] = jnp.full_like(log_in, -1e30)
        state_in[...] = jnp.zeros_like(state_in)
        norm_in[...] = jnp.zeros_like(norm_in)

    norm[...] = jnp.zeros_like(norm)
    both = 2 * rows
    row_at = lax.broadcasted_iota(jnp.int32, (both, both), 0)
    col_at = lax.broadcasted_iota(jnp.int32, (both, both), 1)
    causal = col_at <= row_at
    bias[0] = jnp.where(causal, 0.0, -1e30)
    bias[1] = jnp.where(causal, -1e30, 0.0)
    x_lk().wait_recv()
    x_lq().wait_recv()

    ones = jnp.ones((both, dim), BF16)
    lane = lax.broadcasted_iota(jnp.int32, (both, lanes), 1) // FEAT
    feat_row = lax.broadcasted_iota(jnp.int32, (FEATS, both), 0)
    row_left = jnp.where(feat_row == ONE_ROW, 1.0, 0.0)
    row_right = jnp.where((feat_row >= PAIRS) & (feat_row <= ONE_ROW), 1.0, 0.0)
    norm_lane = lax.broadcasted_iota(jnp.int32, (FEATS, 128), 1)

    feat_lane = lax.broadcasted_iota(jnp.int32, (both, FEATS), 1)
    lane_left = jnp.where(feat_lane == ONE_ROW, 1.0, 0.0)
    lane_right = jnp.where((feat_lane >= PAIRS) & (feat_lane <= ONE_ROW), 2.0, 0.0)

    def first(c, carry):
        x_v(c).wait_recv()
        todo = range(per)
        keys = lk2[...]
        head = [c * per + u for u in todo]
        at = [pl.ds(pl.multiple_of(head[u] * dim, dim), dim) for u in todo]
        key_m = [jnp.where(lane == head[u], keys.astype(F32), 0.0).astype(BF16) for u in todo]
        query_m = [jnp.where(lane == head[u], lq2[...].astype(F32) * 0.25, 0.0).astype(BF16) for u in todo]
        values = [jnp.concatenate([v2[:, at[u]], ones], axis=1) for u in todo]
        left = [dot_t(sel_ref[0], key_m[u]) for u in todo]
        right = [dot_t(sel_ref[1], key_m[u]) for u in todo]
        a = [dot_t(query_m[u], keys) + 1.0 for u in todo]
        feats = [((left[u] + row_left) * (right[u] + row_right)).astype(BF16) for u in todo]
        summed = [dot(feats[u], values[u]) for u in todo]
        weight = [jnp.where(causal, a[u] * a[u] + 1.0, 0.0).astype(BF16) for u in todo]
        mixed = [dot(weight[u], values[u]) for u in todo]
        for u in todo:
            state[head[u]] = summed[u][:, :dim]
            norm[...] += jnp.where(norm_lane == head[u], summed[u][:, dim:], 0.0)

        @pl.when(has_next & (pair == 0))
        def _():
            for u in todo:
                state_out[c, u] = summed[u][:, :dim].astype(state_out.dtype)
            c_state(c).start()

        left = [dot_t(query_m[u], sel_ref[0]) for u in todo]
        right = [dot_t(query_m[u], sel_ref[2]) for u in todo]
        for u in todo:
            num[:, at[u]] = mixed[u][:, :dim]
            den[:, at[u]] = mixed[u][:, dim:]
            qf[head[u]] = ((left[u] + lane_left) * (right[u] + lane_right)).astype(BF16)
        return carry

    lax.fori_loop(0, CHUNKS, first, 0)

    def chain(c):
        c_state(c).wait_recv()
        total = state_in[c].astype(F32) + state[pl.ds(c * per, per)]
        state_out[c] = total.astype(state_out.dtype)
        c_state(c).start()

    def chain_norm():
        c_norm().wait_recv()
        norm_out[...] = norm_in[...] + norm[...]
        c_norm().start()

    @pl.when(has_next & (pair == 0))
    def _():
        norm_out[...] = norm[...]
        c_norm().start()

    early = CHUNKS // 2
    for c in range(CHUNKS):
        x_q(c).wait_recv()

        @pl.when(has_prev)
        def _():
            y_q(c).start()

        @pl.when(has_next & (pair == 1))
        def _():
            chain(c)
            if c == 1:
                chain_norm()

    @pl.when(has_next & (pair >= 2))
    def _():
        for c in range(early):
            chain(c)
        chain_norm()

    factor = dim ** -0.5 * 1.4426950408889634
    head_lane = lax.broadcasted_iota(jnp.int32, (both, 128), 1)
    todo = range(per)

    def heads_at(c):
        head = [c * per + u for u in todo]
        return head, [pl.ds(pl.multiple_of(head[u] * dim, dim), dim) for u in todo]

    def attend(queries, at, which):
        scores = [dot_t(queries[:, at[u]], k2[:, at[u]]) for u in todo]
        scores = [scores[u] * factor + bias[which] for u in todo]
        largest = [jnp.max(scores[u], axis=1, keepdims=True) for u in todo]
        weights = [jnp.exp2(scores[u] - largest[u]).astype(BF16) for u in todo]
        mixed = [dot(weights[u], jnp.concatenate([v2[:, at[u]], ones], axis=1)) for u in todo]
        outs = [mixed[u][:, :dim] / mixed[u][:, dim:] for u in todo]
        return outs, [largest[u] + jnp.log2(mixed[u][:, dim:]) for u in todo]

    def merge(c):
        @pl.when(has_prev)
        def _():
            p_out(c).wait_recv()
            p_log(c).wait_recv()

        head, at = heads_at(c)
        spread = jnp.transpose(jnp.concatenate([log_in[c], jnp.zeros((120, both), F32)], axis=0))
        for u in todo:
            share = 1.0 / (1.0 + jnp.exp2(own_log[:, at[u]] - spread[:, u : u + 1]))
            mine_out = own[:, at[u]]
            win_b[:, at[u]] = (mine_out + (part_in[:, at[u]].astype(F32) - mine_out) * share).astype(BF16)
        r_win(c).start()
        l_win(c).start()

    def second(c, carry):
        x_k(c).wait_recv()

        head, at = heads_at(c)
        @pl.when(has_next)
        def _():
            z_q(c).wait_recv()
            y_q(c).wait_recv()
            outs, logs = attend(qn, at, 1)
            packed = jnp.zeros((both, 128), F32)
            for u in todo:
                part_out[:, at[u]] = outs[u].astype(BF16)
                packed = jnp.where(head_lane == u, logs[u], packed)
            log_out[c] = jnp.transpose(packed)[:8]
            p_out(c).start()
            p_log(c).start()

        outs, logs = attend(q2, at, 0)

        last_pair = has_prev & (pair == pairs - 1)

        @pl.when(last_pair)
        def _():
            c_state(c).wait_recv()

        @pl.when(last_pair & (c == 0))
        def _():
            c_norm().wait_recv()

        added = []
        for u in todo:
            norm_col = jnp.sum(jnp.where(norm_lane == head[u], norm_in[...], 0.0), axis=1, keepdims=True)
            prior = jnp.concatenate(
                [state_in[c, u].astype(BF16), jnp.broadcast_to(norm_col, (FEATS, dim)).astype(BF16)], axis=1
            )
            added.append(dot(qf[head[u]], prior))
        for u in todo:
            own[:, at[u]] = outs[u]
            own_log[:, at[u]] = logs[u]
            linear = (num[:, at[u]] + added[u][:, :dim]) / (den[:, at[u]] + added[u][:, dim:])
            lin_b[:, at[u]] = linear.astype(BF16)
        r_lin(c).start()
        l_lin(c).start()

        @pl.when(has_next & (pair >= 2) & (c == 0))
        def _():
            for late in range(early, CHUNKS):
                chain(late)

        @pl.when(c > 0)
        def _():
            merge(c - 1)

        return carry

    lax.fori_loop(0, CHUNKS, second, 0)

    merge(CHUNKS - 1)

    def last(c, carry):
        r_lin(c).wait_recv()
        r_win(c).wait_recv()
        l_lin(c).wait()
        l_win(c).wait()
        return carry

    lax.fori_loop(0, CHUNKS, last, 0)

    x_lk().wait_send()
    x_lq().wait_send()
    for c in range(CHUNKS):
        x_v(c).wait_send()
        x_k(c).wait_send()
        x_q(c).wait_send()
        r_lin(c).wait_send()
        r_win(c).wait_send()

    @pl.when(has_prev)
    def _():
        for c in range(CHUNKS):
            z_q(c).wait_send()
            y_q(c).wait_send()

    @pl.when(has_next)
    def _():
        c_norm().wait_send()
        for c in range(CHUNKS):
            c_state(c).wait_send()
            p_out(c).wait_send()
            p_log(c).wait_send()


def on_device(linear_query, linear_key, values, window_query, window_key):
    rows, width = values.shape
    heads = linear_query.shape[1] // FEAT
    dim = width // heads
    pairs = lax.axis_size("seq") // 2
    half_heads = heads // 2
    half = width // 2
    lanes = half_heads * FEAT
    both = 2 * rows
    per = half_heads // CHUNKS
    state_type = BF16 if pairs <= 8 else F32
    dma = pltpu.SemaphoreType.DMA
    linear, window = pl.pallas_call(
        functools.partial(kernel, pairs, rows, dim, heads),
        out_shape=(
            jax.ShapeDtypeStruct((rows, width), BF16),
            jax.ShapeDtypeStruct((rows, width), BF16),
        ),
        in_specs=[pl.BlockSpec(memory_space=pl.ANY)] * 6,
        out_specs=(pl.BlockSpec(memory_space=pl.ANY),) * 2,
        scratch_shapes=[
            pltpu.VMEM((3, FEATS, lanes), BF16),
            pltpu.VMEM((rows, lanes), BF16),
            pltpu.VMEM((rows, lanes), BF16),
            pltpu.VMEM((rows, half), BF16),
            pltpu.VMEM((rows, half), BF16),
            pltpu.VMEM((rows, half), BF16),
            pltpu.VMEM((half_heads, both, FEATS), BF16),
            pltpu.VMEM((both, lanes), BF16),
            pltpu.VMEM((both, lanes), BF16),
            pltpu.VMEM((both, half), BF16),
            pltpu.VMEM((both, half), BF16),
            pltpu.VMEM((both, half), BF16),
            pltpu.VMEM((both, half), BF16),
            pltpu.VMEM((both, half), BF16),
            pltpu.VMEM((both, half), BF16),
            pltpu.VMEM((CHUNKS, 8, both), F32),
            pltpu.VMEM((CHUNKS, 8, both), F32),
            pltpu.VMEM((both, half), F32),
            pltpu.VMEM((both, half), F32),
            pltpu.VMEM((both, half), F32),
            pltpu.VMEM((both, half), F32),
            pltpu.VMEM((half_heads, FEATS, dim), F32),
            pltpu.VMEM((FEATS, 128), F32),
            pltpu.VMEM((CHUNKS, per, FEATS, dim), state_type),
            pltpu.VMEM((FEATS, 128), F32),
            pltpu.VMEM((CHUNKS, per, FEATS, dim), state_type),
            pltpu.VMEM((FEATS, 128), F32),
            pltpu.VMEM((both, half), BF16),
            pltpu.VMEM((both, half), BF16),
            pltpu.VMEM((2, both, both), F32),
            dma((2 + 3 * CHUNKS,)),
            dma((2 + 3 * CHUNKS,)),
            dma((2 * CHUNKS,)),
            dma((2 * CHUNKS,)),
            dma((2 * CHUNKS,)),
            dma((2 * CHUNKS,)),
            dma((CHUNKS + 1,)),
            dma((CHUNKS + 1,)),
            dma((2 * CHUNKS,)),
            dma((2 * CHUNKS,)),
            dma((11 + 2 * CHUNKS,)),
        ],
        compiler_params=pltpu.CompilerParams(
            collective_id=0, has_side_effects=True, vmem_limit_bytes=60 * 1024 * 1024
        ),
        cost_estimate=pl.CostEstimate(
            flops=4_000_000_000, bytes_accessed=4_000_000, transcendentals=1_600_000
        ),
    )(linear_query, linear_key, values, window_query, window_key, selections(lanes))
    return linear.astype(F32), window


def solution(mesh):
    spec = P(("grp", "seq"), None)
    return jax.shard_map(
        on_device,
        mesh=mesh,
        in_specs=(spec,) * 5,
        out_specs=(spec, spec),
        check_vma=False,
    )
```
